128 devices in a mesh: rows: 16 (over x, y), store: 8 (over z, core).
Axes of the slice: x: 4, y: 4, z: 4, core: 2. Of those that a mesh axis runs over, the one named last changes fastest.
Arguments:
- stored: float32 [128, 1048576], P('store', 'rows'), as said below
- snap_slot: int32 [64], replicated, may hold values from 0 to 127, as said below
Outputs:
- modes: float32 [64, 1048576], P(None, ('rows', 'store'))
- factor: float32 [64, 64], replicated
The draws below stay inside these ranges and needn't reach their ends.
Inputs may be any that keep to these rules, and one draw needn't show every extreme that they name: `snap_slot`: the numbers are distinct slots; slots s * 16 to (s + 1) * 16 - 1 belong to storage owner s. Owners hold uneven numbers of the panel's snapshots; one owner holds exactly 16 of them. `stored`: entries are finite; the panel has full rank.
All inputs are finite; a program needn't handle non-finite values.
Results may differ from the reference program's by a relative error of at most 0.0003.
Values sent between devices are 32-bit elements; how exact they have to be, the bound alone decides.
No kernel may reach another device: no remote copies, remote signals or barrier semaphores. Data moves between devices by JAX's collectives and lax.ppermute only.
A program may use at most 128 MiB of HBM per device.

```python
import math
import jax
import jax.numpy as jnp
from jax import lax

K = 64
CAP = 16
SLOTS = 128
ROWS = 1048576


def draw_snap_slot(key, part):
    key = jax.random.fold_in(key, 1)
    first, second, third = jax.random.split(key, 3)
    owners = SLOTS // CAP
    full_owner = jax.random.randint(first, (), 0, owners)
    places = jnp.arange(SLOTS, dtype=jnp.int32)
    score = jax.random.randint(second, (SLOTS,), 0, 2 ** 18) * 1024 + places
    score = score + jnp.where(places // CAP == full_owner, 2 ** 29, 0).astype(jnp.int32)
    unused, chosen = lax.top_k(score, K)
    return jax.random.permutation(third, chosen.astype(jnp.int32)).astype(jnp.int32)


def draw_stored(key, part):
    key = jax.random.fold_in(key, 2)
    k_row, k_common, k_noise, k_scale, k_weight, k_second, k_third, k_load_two, k_load_three = jax.random.split(key, 9)
    second_mode = jax.random.normal(k_second, (1, ROWS), jnp.float32)
    third_mode = jax.random.normal(k_third, (1, ROWS), jnp.float32)
    row_scale = jnp.exp(jax.random.uniform(k_row, (1, ROWS), jnp.float32) * math.log(10.0))
    common = jax.random.normal(k_common, (1, ROWS), jnp.float32)
    weight = jax.random.uniform(k_weight, (SLOTS, 1), jnp.float32, 1.0, 2.0)
    load_two = jax.random.uniform(k_load_two, (SLOTS, 1), jnp.float32, -0.3, 0.3)
    load_three = jax.random.uniform(k_load_three, (SLOTS, 1), jnp.float32, -0.05, 0.05)
    noise = jax.random.normal(k_noise, (SLOTS, ROWS), jnp.float32) * 0.03
    slot_scale = jnp.exp(jax.random.uniform(k_scale, (SLOTS, 1), jnp.float32, math.log(0.5), math.log(2.0)))
    shared = weight * common + load_two * second_mode + load_three * third_mode
    return (row_scale * slot_scale * (shared + noise)).astype(jnp.float32)


def setup_inputs(seed: int = 0) -> dict:
    keys = jax.random.split(jax.random.key(seed), 3)
    stored = draw_stored(jax.random.fold_in(keys[2], 71), 0)
    snap_slot = draw_snap_slot(jax.random.fold_in(keys[2], 71), 0)
    return dict(stored=stored, snap_slot=snap_slot)


def upper_factor(gram):
    return jnp.linalg.cholesky(gram).T

def reference(stored, snap_slot):
    panel = jnp.take(stored, snap_slot.astype(jnp.int32), axis=0)
    gram_first = jnp.dot(panel.astype(jnp.float32), panel.T.astype(jnp.float32), precision=lax.Precision.HIGHEST, preferred_element_type=jnp.float32)
    r_first = upper_factor(gram_first)
    basis = jax.scipy.linalg.solve_triangular(r_first.T, panel, lower=True)
    gram_second = jnp.dot(basis.astype(jnp.float32), basis.T.astype(jnp.float32), precision=lax.Precision.HIGHEST, preferred_element_type=jnp.float32)
    r_second = upper_factor(gram_second)
    scale = math.sqrt(ROWS)
    modes = jax.scipy.linalg.solve_triangular(r_second.T, basis, lower=True) * scale
    factor = jnp.dot(r_second.astype(jnp.float32), r_first.astype(jnp.float32), precision=lax.Precision.HIGHEST, preferred_element_type=jnp.float32) / scale
    return (modes, factor)
```

```python
import math

import jax
import jax.numpy as jnp
from jax import lax
from jax.experimental import pallas as pl
from jax.experimental.pallas import tpu as pltpu
from jax.sharding import PartitionSpec as P

HIGHEST = lax.Precision.HIGHEST


def dot(a, b):
    return jnp.dot(a, b, precision=HIGHEST, preferred_element_type=jnp.float32)


def neighbour_sum(value):
    for axis, masks in (("store", (1, 2, 6)), ("rows", (1, 3, 4, 12))):
        for mask in masks:
            pairs = [(i, i ^ mask) for i in range(lax.axis_size(axis))]
            value = value + lax.ppermute(value, axis, pairs)
    return value


def eliminate(gram):
    n = gram.shape[0]
    rows = lax.broadcasted_iota(jnp.int32, (n, n), 0)
    columns = lax.broadcasted_iota(jnp.int32, (n, n), 1)
    whole = jnp.concatenate([gram, (rows == columns).astype(jnp.float32)], axis=1)
    below = lax.broadcasted_iota(jnp.int32, (8, 1), 0)
    blocks = [whole[8 * i : 8 * i + 8] for i in range(n // 8)]
    scales = []
    for j in range(n):
        b, s = divmod(j, 8)
        row = blocks[b][s : s + 1]
        pivot = row[:, j : j + 1]
        scales.append(lax.rsqrt(pivot))
        scaled = row / pivot
        for i in range(b, n // 8):
            column = blocks[i][:, j : j + 1]
            if i == b:
                column = jnp.where(below > s, column, 0.0)
            blocks[i] = blocks[i] - column * scaled
    diagonal = jnp.concatenate(
        [blocks[j // 8][j % 8 : j % 8 + 1, j : j + 1] for j in range(n)], axis=0
    )
    scale = jnp.concatenate(scales, axis=0)
    scale = scale * (1.5 - 0.5 * diagonal * scale * scale)
    whole = jnp.concatenate(blocks, axis=0) * scale
    upper = jnp.where(rows <= columns, whole[:, :n], 0.0)
    lower = jnp.where(rows >= columns, whole[:, n:], 0.0)
    return upper, lower


def factor_kernel(gram_ref, upper_ref, lower_ref):
    upper, lower = eliminate(gram_ref[...])
    upper_ref[...] = upper
    lower_ref[...] = lower


def factor_of(gram):
    shape = jax.ShapeDtypeStruct(gram.shape, jnp.float32)
    return pl.pallas_call(factor_kernel, out_shape=(shape, shape))(gram)


def per_device(stored, snap_slot):
    received = lax.all_to_all(stored, "store", split_axis=1, concat_axis=0, tiled=True)
    places = jnp.arange(received.shape[0], dtype=jnp.int32)
    selector = (snap_slot[:, None] == places[None, :]).astype(jnp.float32)
    panel = dot(selector, received)
    r_first, inverse_first = factor_of(neighbour_sum(dot(panel, panel.T)))
    basis = dot(inverse_first, panel)
    r_second, inverse_second = factor_of(neighbour_sum(dot(basis, basis.T)))
    scale = math.sqrt(panel.shape[1] * lax.axis_size(("rows", "store")))
    modes = dot(inverse_second * scale, basis)
    factor = dot(r_second, r_first) / scale
    return (modes, factor)


def solution(mesh):
    in_specs = (P("store", "rows"), P())
    out_specs = (P(None, ("rows", "store")), P())
    return jax.shard_map(
        per_device, mesh=mesh, in_specs=in_specs, out_specs=out_specs, check_vma=False
    )
```

```python
import math

import jax
import jax.numpy as jnp
from jax import lax
from jax.experimental import pallas as pl
from jax.experimental.pallas import tpu as pltpu
from jax.sharding import PartitionSpec as P

HIGHEST = lax.Precision.HIGHEST
UP = 2.0**24


def dot(a, b):
    return jnp.dot(a, b, precision=HIGHEST, preferred_element_type=jnp.float32)


def iota(shape, dim):
    return lax.broadcasted_iota(jnp.int32, shape, dim)


def power_above(value):
    c, inverse = jnp.ones_like(value), jnp.ones_like(value)
    for e in (64, 32, 16, 8, 4, 2, 1):
        big = value * inverse > 2.0**e * 0.5
        c = jnp.where(big, c * 2.0**e, c)
        inverse = jnp.where(big, inverse * 2.0**-e, inverse)
    for e in (64, 32, 16, 8, 4, 2, 1):
        small = (value * inverse <= 2.0**-e) & (c > 2.0 ** (e - 126))
        c = jnp.where(small, c * 2.0**-e, c)
        inverse = jnp.where(small, inverse * 2.0**e, inverse)
    return c, inverse


def row_of(column):
    n = column.shape[0]
    return jnp.sum(jnp.where(iota((n, n), 0) == iota((n, n), 1), column, 0.0), axis=0, keepdims=True)


def two_sum(a, b):
    s = a + b
    t = s - a
    return s, (a - (s - t)) + (b - t)


def pair_add(first, second):
    s, e = two_sum(first[0], second[0])
    return s, (first[1] + second[1]) + e * UP


def nearest(x):
    return lax.round(x, lax.RoundingMethod.TO_NEAREST_EVEN)


def pieces(x, count):
    out = []
    t = x * 256.0
    for i in range(count):
        n = nearest(t)
        out.append(n)
        t = (t - n) * 512.0
    return out, t


def levels_to_pair(levels):
    hi, lo = levels[0], jnp.zeros_like(levels[0])
    for l in range(1, len(levels)):
        hi, e = two_sum(hi, levels[l] * 2.0 ** (-9 * l))
        lo = lo + e
    return two_sum(hi, lo)


def eliminate(gram, block=8):
    n = gram.shape[0]
    rows, columns = iota((n, n), 0), iota((n, n), 1)
    whole = jnp.concatenate([gram, (rows == columns).astype(jnp.float32)], axis=1)
    lane = iota((8, 2 * n), 1)
    sub = iota((8, 2 * n), 0)
    g = n // 8
    blocks = [whole[8 * i : 8 * i + 8] for i in range(g)]
    done = []
    for b in range(g):
        cols = {}
        for i in range(b, g):
            for q in range(8):
                j = 8 * b + q
                cols[i, q] = jnp.broadcast_to(blocks[i][:, j : j + 1], (8, 2 * n))
        mult = {}
        pivots = jnp.ones((8, 2 * n), jnp.float32)
        rowsb = blocks[b]
        for q in range(8):
            pivot = jnp.broadcast_to(cols[b, q][q : q + 1], (8, 2 * n))
            pivots = jnp.where(sub == q, pivot, pivots)
            w = 1.0 / pivot
            row = jnp.broadcast_to(rowsb[q : q + 1], (8, 2 * n))
            for i in range(b, g):
                m = cols[i, q] * w
                if i == b:
                    m = jnp.where(sub > q, m, 0.0)
                mult[i, q] = m
            rowsb = rowsb - mult[b, q] * row
            for r in range(q + 1, 8):
                a = jnp.broadcast_to(cols[b, r][q : q + 1], (8, 2 * n))
                for i in range(b, g):
                    cols[i, r] = cols[i, r] - mult[i, q] * a
        for i in range(b + 1, g):
            value = blocks[i]
            for q in range(8):
                value = value - mult[i, q] * jnp.broadcast_to(rowsb[q : q + 1], (8, 2 * n))
            blocks[i] = value
        s = lax.rsqrt(pivots)
        s = s * (1.5 - 0.5 * pivots * s * s)
        done.append(rowsb * s)
    whole = jnp.concatenate(done, axis=0)
    upper = jnp.where(rows <= columns, whole[:, :n], 0.0)
    lower = jnp.where(rows >= columns, whole[:, n:], 0.0)
    return upper, lower


def bf16_dot(a, b):
    return lax.dot_general(a, b, (((1,), (0,)), ((), ())), preferred_element_type=jnp.float32)


def wide_product(left, right, keep):
    n = left[0].shape[0]
    na, nb = len(left), len(right)
    l = jnp.concatenate([x.astype(jnp.bfloat16) for x in left], axis=0)
    r = jnp.concatenate([x.astype(jnp.bfloat16) for x in right], axis=1)
    m = bf16_dot(l, r)
    out = []
    for lev in range(keep):
        acc = None
        for a in range(na):
            c = lev - a
            if 0 <= c < nb:
                t = m[a * n : (a + 1) * n, c * n : (c + 1) * n]
                acc = t if acc is None else acc + t
        out.append(acc)
    return out


def second_gram(hi, lo, lower):
    first, rest = pieces(hi, 3)
    rest = rest + lo * (2.0 ** (8 + 27) / UP)
    out = []
    for _ in range(3):
        n = nearest(rest)
        out.append(n)
        rest = (rest - n) * 512.0
    g = first + out
    top = jnp.max(jnp.abs(lower), axis=1, keepdims=True)
    u, v = power_above(top)
    ls, _ = pieces(lower * v, 4)
    lt = [x.T for x in ls]
    ur = row_of(u)
    lev = wide_product(g, lt, 7)
    ch, cl = levels_to_pair(lev)
    scale = ur * 2.0**-16
    ch, cl = ch * scale, cl * scale
    cs, rest = pieces(ch * 0.5, 3)
    rest = rest + cl * (0.5 * 2.0 ** (8 + 27))
    for _ in range(2):
        n = nearest(rest)
        cs.append(n)
        rest = (rest - n) * 512.0
    lev = wide_product(ls, cs, 7)
    h, l = levels_to_pair(lev)
    return (h + l) * (u * 2.0**-15)


def finish(hi, lo, count):
    n = hi.shape[0]
    eye = iota((n, n), 0) == iota((n, n), 1)
    diag = jnp.sum(jnp.where(eye, hi, 0.0), axis=1, keepdims=True)
    d, di = power_above(jnp.sqrt(diag))
    dr, dir_ = row_of(d), row_of(di)
    hs = (hi * di) * dir_
    ls = (lo * di) * dir_
    r1, l1 = eliminate(hs)
    g2 = second_gram(hs, ls, l1)
    r2, l2 = eliminate(g2)
    scale = math.sqrt(count)
    w = dot(l2, l1) * (dir_ * scale)
    factor = dot(r2, r1) * (dr * (1.0 / scale))
    return w, factor, g2


def combine(acc, c):
    n = acc.shape[0] // 4
    cr = row_of(c)
    levels = []
    for lev in range(7):
        t = None
        for a in range(4):
            b = lev - a
            if 0 <= b < 4:
                x = acc[a * n : (a + 1) * n, b * n : (b + 1) * n]
                t = x if t is None else t + x
        levels.append(t)
    hi = jnp.zeros((n, n), jnp.float32)
    lo = jnp.zeros((n, n), jnp.float32)
    for lev, t in enumerate(levels):
        high = lax.shift_right_arithmetic(t, 14)
        low = (t - lax.shift_left(high, 14)).astype(jnp.float32) * 2.0 ** (-9 * lev)
        high = high.astype(jnp.float32) * 2.0 ** (14 - 9 * lev)
        hi, e = two_sum(hi, high)
        lo = lo + e
        hi, e = two_sum(hi, low)
        lo = lo + e
    hi, lo = two_sum(hi, lo)
    f = 2.0**-16
    return ((hi * f) * c) * cr, (((lo * (f * UP)) * c) * cr)


STEP = 256


def gram_kernel(panel_ref, out_ref, sum_ref):
    n, columns = panel_ref.shape
    c, inverse = power_above(jnp.max(jnp.abs(panel_ref[...]), axis=1, keepdims=True))
    sum_ref[...] = jnp.zeros_like(sum_ref)

    def step(k, carry):
        block = panel_ref[:, pl.ds(pl.multiple_of(k * STEP, STEP), STEP)]
        parts, _ = pieces(block * inverse, 4)
        x = jnp.concatenate([p.astype(jnp.bfloat16) for p in parts], axis=0)
        h = lax.dot_general(x, x, (((1,), (1,)), ((), ())), preferred_element_type=jnp.float32)
        sum_ref[...] += h.astype(jnp.int32)
        return carry

    lax.fori_loop(0, columns // STEP, step, 0, unroll=4)
    hi, lo = combine(sum_ref[...], c)
    pair = jnp.concatenate([hi, lo], axis=1)
    for i in range(out_ref.shape[0]):
        out_ref[i] = pair


def pair_sum(ref):
    lane = iota(ref.shape[1:], 1)
    half = ref.shape[2] // 2
    total, rest = ref[0], jnp.zeros(ref.shape[1:], jnp.float32)
    for i in range(1, ref.shape[0]):
        total, e = two_sum(total, ref[i])
        rest = rest + e
    rest = jnp.where(lane < half, rest * UP, 0.0)
    return total + pltpu.roll(rest, half, 1)


def sum_kernel(in_ref, out_ref):
    total = pair_sum(in_ref)
    for i in range(out_ref.shape[0]):
        out_ref[i] = total


def finish_kernel(count, in_ref, w_ref, factor_ref):
    total = pair_sum(in_ref)
    n = total.shape[0]
    w, factor, _ = finish(total[:, :n], total[:, n:], count)
    w_ref[...] = w
    factor_ref[...] = factor


def per_device(stored, snap_slot):
    received = lax.all_to_all(stored, "store", split_axis=1, concat_axis=0, tiled=True)
    places = jnp.arange(received.shape[0], dtype=jnp.int32)
    selector = (snap_slot[:, None] == places[None, :]).astype(jnp.float32)
    panel = dot(selector, received)
    n, columns = panel.shape
    store, rows = lax.axis_size("store"), lax.axis_size("rows")
    f32 = jnp.float32
    pairs = pl.pallas_call(
        gram_kernel,
        out_shape=jax.ShapeDtypeStruct((store, n, 2 * n), f32),
        scratch_shapes=[pltpu.VMEM((4 * n, 4 * n), jnp.int32)],
        compiler_params=pltpu.CompilerParams(vmem_limit_bytes=32 * 2**20),
    )(panel)
    pairs = lax.all_to_all(pairs, "store", split_axis=0, concat_axis=0, tiled=True)
    pairs = pl.pallas_call(sum_kernel, out_shape=jax.ShapeDtypeStruct((rows, n, 2 * n), f32))(pairs)
    pairs = lax.all_to_all(pairs, "rows", split_axis=0, concat_axis=0, tiled=True)
    square = jax.ShapeDtypeStruct((n, n), f32)
    weights, factor = pl.pallas_call(
        lambda *refs: finish_kernel(columns * store * rows, *refs), out_shape=(square, square)
    )(pairs)
    return (dot(weights, panel), factor)


def solution(mesh):
    in_specs = (P("store", "rows"), P())
    out_specs = (P(None, ("rows", "store")), P())
    return jax.shard_map(
        per_device, mesh=mesh, in_specs=in_specs, out_specs=out_specs, check_vma=False
    )
```

```python
import math

import jax
import jax.numpy as jnp
from jax import lax
from jax.experimental import pallas as pl
from jax.experimental.pallas import tpu as pltpu
from jax.sharding import PartitionSpec as P

HIGHEST = lax.Precision.HIGHEST
UP = 2.0**24


def dot(a, b):
    return jnp.dot(a, b, precision=HIGHEST, preferred_element_type=jnp.float32)


def iota(shape, dim):
    return lax.broadcasted_iota(jnp.int32, shape, dim)


def power_above(value):
    c, inverse = jnp.ones_like(value), jnp.ones_like(value)
    for e in (64, 32, 16, 8, 4, 2, 1):
        big = value * inverse > 2.0**e * 0.5
        c = jnp.where(big, c * 2.0**e, c)
        inverse = jnp.where(big, inverse * 2.0**-e, inverse)
    for e in (64, 32, 16, 8, 4, 2, 1):
        small = (value * inverse <= 2.0**-e) & (c > 2.0 ** (e - 126))
        c = jnp.where(small, c * 2.0**-e, c)
        inverse = jnp.where(small, inverse * 2.0**e, inverse)
    return c, inverse


def row_of(column):
    n = column.shape[0]
    return jnp.sum(jnp.where(iota((n, n), 0) == iota((n, n), 1), column, 0.0), axis=0, keepdims=True)


def two_sum(a, b):
    s = a + b
    t = s - a
    return s, (a - (s - t)) + (b - t)


def pair_add(first, second):
    s, e = two_sum(first[0], second[0])
    return s, (first[1] + second[1]) + e * UP


def nearest(x):
    return lax.round(x, lax.RoundingMethod.TO_NEAREST_EVEN)


def pieces(x, count):
    out = []
    t = x * 256.0
    for i in range(count):
        n = nearest(t)
        out.append(n)
        t = (t - n) * 512.0
    return out, t


def levels_to_pair(levels):
    hi, lo = levels[0], jnp.zeros_like(levels[0])
    for l in range(1, len(levels)):
        hi, e = two_sum(hi, levels[l] * 2.0 ** (-9 * l))
        lo = lo + e
    return two_sum(hi, lo)


def eliminate(gram, block=8):
    n = gram.shape[0]
    rows, columns = iota((n, n), 0), iota((n, n), 1)
    whole = jnp.concatenate([gram, (rows == columns).astype(jnp.float32)], axis=1)
    lane = iota((8, 2 * n), 1)
    sub = iota((8, 2 * n), 0)
    g = n // 8
    blocks = [whole[8 * i : 8 * i + 8] for i in range(g)]
    done = []
    for b in range(g):
        cols = {}
        for i in range(b, g):
            for q in range(8):
                j = 8 * b + q
                cols[i, q] = jnp.broadcast_to(blocks[i][:, j : j + 1], (8, 2 * n))
        mult = {}
        pivots = jnp.ones((8, 2 * n), jnp.float32)
        rowsb = blocks[b]
        for q in range(8):
            pivot = jnp.broadcast_to(cols[b, q][q : q + 1], (8, 2 * n))
            pivots = jnp.where(sub == q, pivot, pivots)
            w = 1.0 / pivot
            row = jnp.broadcast_to(rowsb[q : q + 1], (8, 2 * n))
            for i in range(b, g):
                m = cols[i, q] * w
                if i == b:
                    m = jnp.where(sub > q, m, 0.0)
                mult[i, q] = m
            rowsb = rowsb - mult[b, q] * row
            for r in range(q + 1, 8):
                a = jnp.broadcast_to(cols[b, r][q : q + 1], (8, 2 * n))
                for i in range(b, g):
                    cols[i, r] = cols[i, r] - mult[i, q] * a
        for i in range(b + 1, g):
            value = blocks[i]
            for q in range(8):
                value = value - mult[i, q] * jnp.broadcast_to(rowsb[q : q + 1], (8, 2 * n))
            blocks[i] = value
        s = lax.rsqrt(pivots)
        s = s * (1.5 - 0.5 * pivots * s * s)
        done.append(rowsb * s)
    whole = jnp.concatenate(done, axis=0)
    upper = jnp.where(rows <= columns, whole[:, :n], 0.0)
    lower = jnp.where(rows >= columns, whole[:, n:], 0.0)
    return upper, lower


def bf16_dot(a, b):
    return lax.dot_general(a, b, (((1,), (0,)), ((), ())), preferred_element_type=jnp.float32)


def wide_product(left, right, keep):
    n = left[0].shape[0]
    na, nb = len(left), len(right)
    l = jnp.concatenate([x.astype(jnp.bfloat16) for x in left], axis=0)
    r = jnp.concatenate([x.astype(jnp.bfloat16) for x in right], axis=1)
    m = bf16_dot(l, r)
    out = []
    for lev in range(keep):
        acc = None
        for a in range(na):
            c = lev - a
            if 0 <= c < nb:
                t = m[a * n : (a + 1) * n, c * n : (c + 1) * n]
                acc = t if acc is None else acc + t
        out.append(acc)
    return out


def second_gram(hi, lo, lower):
    first, rest = pieces(hi, 3)
    rest = rest + lo * (2.0 ** (8 + 27) / UP)
    out = []
    for _ in range(3):
        n = nearest(rest)
        out.append(n)
        rest = (rest - n) * 512.0
    g = first + out
    top = jnp.max(jnp.abs(lower), axis=1, keepdims=True)
    u, v = power_above(top)
    ls, _ = pieces(lower * v, 4)
    lt = [x.T for x in ls]
    ur = row_of(u)
    lev = wide_product(g, lt, 7)
    ch, cl = levels_to_pair(lev)
    scale = ur * 2.0**-16
    ch, cl = ch * scale, cl * scale
    cs, rest = pieces(ch * 0.5, 3)
    rest = rest + cl * (0.5 * 2.0 ** (8 + 27))
    for _ in range(2):
        n = nearest(rest)
        cs.append(n)
        rest = (rest - n) * 512.0
    lev = wide_product(ls, cs, 7)
    h, l = levels_to_pair(lev)
    return (h + l) * (u * 2.0**-15)


def finish(hi, lo, count):
    n = hi.shape[0]
    eye = iota((n, n), 0) == iota((n, n), 1)
    diag = jnp.sum(jnp.where(eye, hi, 0.0), axis=1, keepdims=True)
    d, di = power_above(jnp.sqrt(diag))
    dr, dir_ = row_of(d), row_of(di)
    hs = (hi * di) * dir_
    ls = (lo * di) * dir_
    r1, l1 = eliminate(hs)
    g2 = second_gram(hs, ls, l1)
    r2, l2 = eliminate(g2)
    scale = math.sqrt(count)
    w = dot(l2, l1) * (dir_ * scale)
    factor = dot(r2, r1) * (dr * (1.0 / scale))
    return w, factor, g2


def combine(acc, c):
    n = acc.shape[0] // 4
    cr = row_of(c)
    levels = []
    for lev in range(7):
        t = None
        for a in range(4):
            b = lev - a
            if 0 <= b < 4:
                x = acc[a * n : (a + 1) * n, b * n : (b + 1) * n]
                t = x if t is None else t + x
        levels.append(t)
    hi = jnp.zeros((n, n), jnp.float32)
    lo = jnp.zeros((n, n), jnp.float32)
    for lev, t in enumerate(levels):
        high = lax.shift_right_arithmetic(t, 14)
        low = (t - lax.shift_left(high, 14)).astype(jnp.float32) * 2.0 ** (-9 * lev)
        high = high.astype(jnp.float32) * 2.0 ** (14 - 9 * lev)
        hi, e = two_sum(hi, high)
        lo = lo + e
        hi, e = two_sum(hi, low)
        lo = lo + e
    hi, lo = two_sum(hi, lo)
    f = 2.0**-16
    return ((hi * f) * c) * cr, (((lo * (f * UP)) * c) * cr)


STEP = 256
CORES = 2
BIG = pltpu.CompilerParams(vmem_limit_bytes=32 * 2**20)


def thirds(x):
    high = x.astype(jnp.bfloat16)
    rest = x - high.astype(jnp.float32)
    mid = rest.astype(jnp.bfloat16)
    low = (rest - mid.astype(jnp.float32)).astype(jnp.bfloat16)
    return jnp.concatenate([high, mid, low], axis=0)


def place():
    store = lax.axis_index("store")
    return store // CORES, store % CORES


def part_kernel(distances, chips, stored_ref, *refs):
    outs, sems = refs[-1 - len(distances) : -1], refs[-1]
    width = outs[0].shape[1]
    z, core = place()
    copies = []
    for d, out in zip(distances, outs):
        owner = lax.rem(z + d, chips) * CORES + 1 - core
        start = pl.multiple_of(owner * width, width)
        copies.append(pltpu.make_async_copy(stored_ref.at[:, pl.ds(start, width)], out, sems.at[len(copies)]))
    for copy in copies:
        copy.start()
    for copy in copies:
        copy.wait()


def pick_kernel(distance, chips, stored_ref, other_ref, selector_ref, out_ref, own_ref, sem):
    width = out_ref.shape[1]
    z, core = place()
    owner = lax.rem(z + distance, chips) * CORES + core
    start = pl.multiple_of(owner * width, width)
    copy = pltpu.make_async_copy(stored_ref.at[:, pl.ds(start, width)], own_ref, sem)
    copy.start()
    selector = selector_ref[...]
    copy.wait()

    def step(k, carry):
        block = pl.ds(pl.multiple_of(k * STEP, STEP), STEP)
        both = jnp.concatenate([own_ref[:, block], other_ref[:, block]], axis=0)
        out_ref[:, block] = bf16_dot(selector, thirds(both))
        return carry

    lax.fori_loop(0, width // STEP, step, 0, unroll=8)


def gram_kernel(*refs):
    blocks_refs, (selector_ref, panel_ref, out_ref, sum_ref) = refs[:-4], refs[-4:]
    n, columns = panel_ref.shape
    selector = selector_ref[...]

    def gather(k, top):
        block = pl.ds(pl.multiple_of(k * STEP, STEP), STEP)
        got = jnp.concatenate([ref[:, block] for ref in blocks_refs], axis=0)
        rows = bf16_dot(selector, thirds(got))
        panel_ref[:, block] = rows
        return jnp.maximum(top, jnp.abs(rows))

    top = lax.fori_loop(0, columns // STEP, gather, jnp.zeros((n, STEP), jnp.float32), unroll=8)
    c, inverse = power_above(jnp.max(top, axis=1, keepdims=True))
    sum_ref[...] = jnp.zeros_like(sum_ref)

    def step(k, carry):
        block = panel_ref[:, pl.ds(pl.multiple_of(k * STEP, STEP), STEP)]
        parts, _ = pieces(block * inverse, 4)
        x = jnp.concatenate([p.astype(jnp.bfloat16) for p in parts], axis=0)
        h = lax.dot_general(x, x, (((1,), (1,)), ((), ())), preferred_element_type=jnp.float32)
        sum_ref[...] += h.astype(jnp.int32)
        return carry

    lax.fori_loop(0, columns // STEP, step, 0, unroll=4)
    packed = pack(*combine(sum_ref[...], c))
    for i in range(out_ref.shape[0]):
        out_ref[i] = packed


def pack(hi, lo):
    h = hi.shape[0] // 2
    rows, columns = iota((h, h), 0), iota((h, h), 1)
    wide, diagonals = [], []
    for x in (hi, lo):
        a, b, c = x[:h, :h], x[:h, h:], x[h:, h:]
        diagonal = jnp.sum(jnp.where(rows == columns, c, 0.0), axis=0, keepdims=True)
        wide += [jnp.where(columns >= rows, a, c), b]
        diagonals += [diagonal, jnp.zeros_like(diagonal)]
    tail = jnp.broadcast_to(jnp.concatenate(diagonals, axis=1), (8, 4 * h))
    return jnp.concatenate([jnp.concatenate(wide, axis=1), tail], axis=0)


def unpack(packed):
    h = packed.shape[1] // 4
    rows, columns = iota((h, h), 0), iota((h, h), 1)
    main = packed[:h]
    turned = main.T
    out = []
    for i in (0, 2 * h):
        m, mt = main[:, i : i + h], turned[i : i + h]
        b, bt = main[:, i + h : i + 2 * h], turned[i + h : i + 2 * h]
        a = jnp.where(columns >= rows, m, mt)
        c = jnp.where(columns < rows, m, jnp.where(columns > rows, mt, packed[h : h + 1, i : i + h]))
        out.append(jnp.concatenate([jnp.concatenate([a, b], axis=1), jnp.concatenate([bt, c], axis=1)], axis=0))
    return out


def pair_sum(ref):
    lane = iota(ref.shape[1:], 1)
    half = ref.shape[2] // 2
    total, rest = ref[0], jnp.zeros(ref.shape[1:], jnp.float32)
    for i in range(1, ref.shape[0]):
        total, e = two_sum(total, ref[i])
        rest = rest + e
    rest = jnp.where(lane < half, rest * UP, 0.0)
    return total + pltpu.roll(rest, half, 1)


def sum_kernel(in_ref, out_ref):
    total = pair_sum(in_ref)
    for i in range(out_ref.shape[0]):
        out_ref[i] = total


def finish_kernel(count, in_ref, w_ref, factor_ref):
    w, factor, _ = finish(*unpack(pair_sum(in_ref)), count)
    w_ref[...] = w
    factor_ref[...] = factor


def float_array(*shape):
    return jax.ShapeDtypeStruct(shape, jnp.float32)


def modes_kernel(weights_ref, panel_ref, out_ref):
    n = weights_ref.shape[0]
    w = thirds(weights_ref[...])
    first, second, third = w[:n], w[n : 2 * n], w[2 * n :]
    none = jnp.zeros_like(first)
    left = jnp.concatenate(
        [
            jnp.concatenate([first, first, first], axis=1),
            jnp.concatenate([second, second, none], axis=1),
            jnp.concatenate([third, none, none], axis=1),
        ],
        axis=0,
    )

    def step(k, carry):
        block = pl.ds(pl.multiple_of(k * STEP, STEP), STEP)
        got = bf16_dot(left, thirds(panel_ref[:, block]))
        out_ref[:, block] = (got[2 * n :] + got[n : 2 * n]) + got[:n]
        return carry

    lax.fori_loop(0, out_ref.shape[1] // STEP, step, 0, unroll=True)


def swapped(distances, chips, stored, *after):
    store = lax.axis_size("store")
    parts = pl.pallas_call(
        lambda *refs: part_kernel(distances, chips, *refs),
        out_shape=(float_array(stored.shape[0], stored.shape[1] // store),) * len(distances),
        in_specs=[pl.BlockSpec(memory_space=pl.ANY)] * (1 + len(after)),
        scratch_shapes=[pltpu.SemaphoreType.DMA((len(distances),))],
        compiler_params=BIG,
    )(stored, *after)
    swap = [(i, i ^ 1) for i in range(store)]
    return [lax.ppermute(part, "store", swap) for part in parts]


def picked(distance, chips, stored, other, pick):
    slots, width = other.shape
    return pl.pallas_call(
        lambda *refs: pick_kernel(distance, chips, *refs),
        out_shape=float_array(pick.shape[0], width),
        in_specs=[pl.BlockSpec(memory_space=pl.ANY)] + [pl.BlockSpec(memory_space=pltpu.VMEM)] * 2,
        scratch_shapes=[pltpu.VMEM((slots, width), jnp.float32), pltpu.SemaphoreType.DMA(())],
        compiler_params=BIG,
    )(stored, other, pick)


def relayout(capacity, stored, other, pick, chip, position):
    n = chip.shape[0]
    slots, width = other.shape
    store = lax.axis_size("store")
    chips = store // CORES
    z, core = place()
    pick = pick[:capacity]

    def send(block, d):
        return lax.ppermute(block, "store", [(i, (i + d * CORES) % store) for i in range(store)])

    blocks = [None] * chips
    block = picked(2, chips, stored, other, pick)
    blocks[2] = send(block, 2)
    rest = (1, 3, 0)
    for d, other in zip(rest, swapped(rest, chips, stored, block)):
        block = picked(d, chips, stored, other, pick)
        blocks[d] = send(block, d) if d else block
    source = lax.rem(z - chip + chips, chips) * capacity + position
    gather = source[:, None] == jnp.arange(chips * capacity)[None, :]
    gather = jnp.tile(gather.astype(jnp.bfloat16), (1, 3))
    return pl.pallas_call(
        gram_kernel,
        out_shape=(float_array(n, width), float_array(store, n // 2 + 8, 2 * n)),
        scratch_shapes=[pltpu.VMEM((4 * n, 4 * n), jnp.int32)],
        compiler_params=BIG,
    )(*blocks, gather)


def per_device(stored, snap_slot):
    n = snap_slot.shape[0]
    slots = stored.shape[0]
    store, rows = lax.axis_size("store"), lax.axis_size("rows")
    columns, chips = stored.shape[1] // store, store // CORES
    (other,) = swapped((2,), chips, stored)
    z, core = place()
    chip = snap_slot // (slots * CORES)
    same = chip[:, None] == chip[None, :]
    position = jnp.sum((same & (snap_slot[None, :] < snap_slot[:, None])).astype(jnp.int32), axis=1)
    most = jnp.max(position) + 1
    capacities = (16, 24, 32)
    choice = sum((most > c).astype(jnp.int32) for c in capacities[:-1])
    local = snap_slot - (chip * CORES + core) * slots
    local = jnp.where(local < 0, local + 2 * slots, local)
    order = jnp.arange(2 * slots)
    chosen = (chip == z)[None, :] & (position[None, :] == order[:, None])
    pick = jnp.any(chosen[:, None, :] & (local[None, None, :] == order[None, :, None]), axis=2)
    pick = jnp.tile(pick.astype(jnp.bfloat16), (1, 3))
    branches = [lambda *args, c=c: relayout(c, *args) for c in capacities]
    panel, pairs = lax.switch(choice, branches, stored, other, pick, chip, position)
    pairs = lax.all_to_all(pairs, "store", split_axis=0, concat_axis=0, tiled=True)
    pairs = pl.pallas_call(sum_kernel, out_shape=float_array(rows, n // 2 + 8, 2 * n))(pairs)
    pairs = lax.all_to_all(pairs, "rows", split_axis=0, concat_axis=0, tiled=True)
    weights, factor = pl.pallas_call(
        lambda *refs: finish_kernel(columns * store * rows, *refs),
        out_shape=(float_array(n, n),) * 2,
    )(pairs)
    wide = columns // 4
    modes = pl.pallas_call(
        modes_kernel,
        grid=(columns // wide,),
        out_shape=float_array(n, columns),
        in_specs=[pl.BlockSpec((n, n), lambda i: (0, 0)), pl.BlockSpec((n, wide), lambda i: (0, i))],
        out_specs=pl.BlockSpec((n, wide), lambda i: (0, i)),
        compiler_params=BIG,
    )(weights, panel)
    return (modes, factor)


def solution(mesh):
    in_specs = (P("store", "rows"), P())
    out_specs = (P(None, ("rows", "store")), P())
    return jax.shard_map(
        per_device, mesh=mesh, in_specs=in_specs, out_specs=out_specs, check_vma=False
    )
```

```python
import math

import jax
import jax.numpy as jnp
from jax import lax
from jax.experimental import pallas as pl
from jax.experimental.pallas import tpu as pltpu
from jax.sharding import PartitionSpec as P

HIGHEST = lax.Precision.HIGHEST
UP = 2.0**24


def dot(a, b):
    return jnp.dot(a, b, precision=HIGHEST, preferred_element_type=jnp.float32)


def iota(shape, dim):
    return lax.broadcasted_iota(jnp.int32, shape, dim)


def power_above(value):
    c, inverse = jnp.ones_like(value), jnp.ones_like(value)
    for e in (64, 32, 16, 8, 4, 2, 1):
        big = value * inverse > 2.0**e * 0.5
        c = jnp.where(big, c * 2.0**e, c)
        inverse = jnp.where(big, inverse * 2.0**-e, inverse)
    for e in (64, 32, 16, 8, 4, 2, 1):
        small = (value * inverse <= 2.0**-e) & (c > 2.0 ** (e - 126))
        c = jnp.where(small, c * 2.0**-e, c)
        inverse = jnp.where(small, inverse * 2.0**e, inverse)
    return c, inverse


def row_of(column):
    n = column.shape[0]
    return jnp.sum(jnp.where(iota((n, n), 0) == iota((n, n), 1), column, 0.0), axis=0, keepdims=True)


def two_sum(a, b):
    s = a + b
    t = s - a
    return s, (a - (s - t)) + (b - t)


def pair_add(first, second):
    s, e = two_sum(first[0], second[0])
    return s, (first[1] + second[1]) + e * UP


def nearest(x):
    return lax.round(x, lax.RoundingMethod.TO_NEAREST_EVEN)


def pieces(x, count):
    out = []
    t = x * 256.0
    for i in range(count):
        n = nearest(t)
        out.append(n)
        t = (t - n) * 512.0
    return out, t


def levels_to_pair(levels):
    hi, lo = levels[0], jnp.zeros_like(levels[0])
    for l in range(1, len(levels)):
        hi, e = two_sum(hi, levels[l] * 2.0 ** (-9 * l))
        lo = lo + e
    return two_sum(hi, lo)


def eliminate(gram, block=8):
    n = gram.shape[0]
    rows, columns = iota((n, n), 0), iota((n, n), 1)
    whole = jnp.concatenate([gram, (rows == columns).astype(jnp.float32)], axis=1)
    lane = iota((8, 2 * n), 1)
    sub = iota((8, 2 * n), 0)
    g = n // 8
    blocks = [whole[8 * i : 8 * i + 8] for i in range(g)]
    done = []
    for b in range(g):
        cols = {}
        for i in range(b, g):
            for q in range(8):
                j = 8 * b + q
                cols[i, q] = jnp.broadcast_to(blocks[i][:, j : j + 1], (8, 2 * n))
        mult = {}
        pivots = jnp.ones((8, 2 * n), jnp.float32)
        rowsb = blocks[b]
        for q in range(8):
            pivot = jnp.broadcast_to(cols[b, q][q : q + 1], (8, 2 * n))
            pivots = jnp.where(sub == q, pivot, pivots)
            w = 1.0 / pivot
            row = jnp.broadcast_to(rowsb[q : q + 1], (8, 2 * n))
            for i in range(b, g):
                m = cols[i, q] * w
                if i == b:
                    m = jnp.where(sub > q, m, 0.0)
                mult[i, q] = m
            rowsb = rowsb - mult[b, q] * row
            for r in range(q + 1, 8):
                a = jnp.broadcast_to(cols[b, r][q : q + 1], (8, 2 * n))
                for i in range(b, g):
                    cols[i, r] = cols[i, r] - mult[i, q] * a
        for i in range(b + 1, g):
            value = blocks[i]
            for q in range(8):
                value = value - mult[i, q] * jnp.broadcast_to(rowsb[q : q + 1], (8, 2 * n))
            blocks[i] = value
        s = lax.rsqrt(pivots)
        s = s * (1.5 - 0.5 * pivots * s * s)
        done.append(rowsb * s)
    whole = jnp.concatenate(done, axis=0)
    upper = jnp.where(rows <= columns, whole[:, :n], 0.0)
    lower = jnp.where(rows >= columns, whole[:, n:], 0.0)
    return upper, lower


def bf16_dot(a, b):
    return lax.dot_general(a, b, (((1,), (0,)), ((), ())), preferred_element_type=jnp.float32)


def wide_product(left, right, keep):
    n = left[0].shape[0]
    na, nb = len(left), len(right)
    l = jnp.concatenate([x.astype(jnp.bfloat16) for x in left], axis=0)
    r = jnp.concatenate([x.astype(jnp.bfloat16) for x in right], axis=1)
    m = bf16_dot(l, r)
    out = []
    for lev in range(keep):
        acc = None
        for a in range(na):
            c = lev - a
            if 0 <= c < nb:
                t = m[a * n : (a + 1) * n, c * n : (c + 1) * n]
                acc = t if acc is None else acc + t
        out.append(acc)
    return out


def second_gram(hi, lo, lower):
    first, rest = pieces(hi, 3)
    rest = rest + lo * (2.0 ** (8 + 27) / UP)
    out = []
    for _ in range(3):
        n = nearest(rest)
        out.append(n)
        rest = (rest - n) * 512.0
    g = first + out
    top = jnp.max(jnp.abs(lower), axis=1, keepdims=True)
    u, v = power_above(top)
    ls, _ = pieces(lower * v, 4)
    lt = [x.T for x in ls]
    ur = row_of(u)
    lev = wide_product(g, lt, 7)
    ch, cl = levels_to_pair(lev)
    scale = ur * 2.0**-16
    ch, cl = ch * scale, cl * scale
    cs, rest = pieces(ch * 0.5, 3)
    rest = rest + cl * (0.5 * 2.0 ** (8 + 27))
    for _ in range(2):
        n = nearest(rest)
        cs.append(n)
        rest = (rest - n) * 512.0
    lev = wide_product(ls, cs, 7)
    h, l = levels_to_pair(lev)
    return (h + l) * (u * 2.0**-15)


def finish(hi, lo, count):
    n = hi.shape[0]
    eye = iota((n, n), 0) == iota((n, n), 1)
    diag = jnp.sum(jnp.where(eye, hi, 0.0), axis=1, keepdims=True)
    d, di = power_above(jnp.sqrt(diag))
    dr, dir_ = row_of(d), row_of(di)
    hs = (hi * di) * dir_
    ls = (lo * di) * dir_
    r1, l1 = eliminate(hs)
    g2 = second_gram(hs, ls, l1)
    r2, l2 = eliminate(g2)
    scale = math.sqrt(count)
    w = dot(l2, l1) * (dir_ * scale)
    factor = dot(r2, r1) * (dr * (1.0 / scale))
    return w, factor, g2


def combine(acc, c):
    n = acc.shape[0] // 2
    cr = row_of(c)
    part = [[acc[a * n : (a + 1) * n, b * n : (b + 1) * n] for b in range(4)] for a in range(2)]
    levels = [part[0][0], part[0][1] + part[1][0]]
    levels.append(part[0][2] + part[0][2].T + part[1][1])
    last = part[0][3] + part[1][2]
    levels.append(last + last.T)
    hi = jnp.zeros((n, n), jnp.float32)
    lo = jnp.zeros((n, n), jnp.float32)
    for lev, t in enumerate(levels):
        high = lax.shift_right_arithmetic(t, 14)
        low = (t - lax.shift_left(high, 14)).astype(jnp.float32) * 2.0 ** (-9 * lev)
        high = high.astype(jnp.float32) * 2.0 ** (14 - 9 * lev)
        hi, e = two_sum(hi, high)
        lo = lo + e
        hi, e = two_sum(hi, low)
        lo = lo + e
    hi, lo = two_sum(hi, lo)
    f = 2.0**-16
    return ((hi * f) * c) * cr, (((lo * (f * UP)) * c) * cr)


STEP = 256
CORES = 2
QUARTERS = 4
BIG = pltpu.CompilerParams(vmem_limit_bytes=16 * 2**20)
ANY = pl.BlockSpec(memory_space=pl.ANY)
HBM = pl.BlockSpec(memory_space=pltpu.HBM)
VMEM = pl.BlockSpec(memory_space=pltpu.VMEM)


def thirds(x):
    high = x.astype(jnp.bfloat16)
    rest = x - high.astype(jnp.float32)
    mid = rest.astype(jnp.bfloat16)
    low = (rest - mid.astype(jnp.float32)).astype(jnp.bfloat16)
    return jnp.concatenate([high, mid, low], axis=0)


def place():
    store = lax.axis_index("store")
    return store // CORES, store % CORES


def row_sum(mask_value):
    return jnp.sum(mask_value, axis=0, keepdims=True)


def positions(slot, span):
    n = slot.shape[1]
    column = jnp.sum(jnp.where(iota((n, n), 0) == iota((n, n), 1), slot, 0), axis=1, keepdims=True)
    before = (column < slot) & (column // span == slot // span)
    return slot // span, row_sum(before.astype(jnp.int32))


def part_kernel(distance, chips, stored_ref, out_ref, sem):
    columns = out_ref.shape[1]
    z, core = place()
    owner = lax.rem(z + distance, chips) * CORES + 1 - core
    start = pl.multiple_of(owner * columns, columns)
    copy = pltpu.make_async_copy(stored_ref.at[:, pl.ds(start, columns)], out_ref, sem)
    copy.start()
    copy.wait()


def pick_kernel(distance, passed, chips, capacity, stored_ref, slot_ref, other_ref, *refs):
    out, part_refs, both_ref, sems = refs[-3 - len(passed)], refs[-2 - len(passed) : -2], refs[-2], refs[-1]
    slots, columns = other_ref.shape
    z, core = place()

    def part(d, c):
        owner = lax.rem(z + d, chips) * CORES + c
        return stored_ref.at[:, pl.ds(pl.multiple_of(owner * columns, columns), columns)]

    copies = [
        pltpu.make_async_copy(part(distance, core), both_ref.at[pl.ds(0, slots)], sems.at[0]),
        pltpu.make_async_copy(other_ref, both_ref.at[pl.ds(slots, slots)], sems.at[1]),
    ]
    for i, d in enumerate(passed):
        copies.append(pltpu.make_async_copy(part(d, 1 - core), part_refs[i], sems.at[2 + i]))
    for copy in copies:
        copy.start()
    slot = slot_ref[...]
    span = CORES * slots
    chip, position = positions(slot, span)
    local = slot - (chip * CORES + core) * slots
    local = jnp.where(local < 0, local + span, local)
    count = slot.shape[1]
    rows = QUARTERS * capacity
    row, column = iota((rows, count), 0), iota((span, count), 0)
    quarter = sum((row >= q * capacity).astype(jnp.int32) for q in range(1, QUARTERS))
    ranks = ((chip == z) & (position == row - quarter * capacity)).astype(jnp.bfloat16)
    locals_ = (local == column).astype(jnp.bfloat16)
    locals_ = jnp.concatenate([locals_] * QUARTERS, axis=0)
    hit = lax.dot_general(ranks, locals_, (((1,), (1,)), ((), ())), preferred_element_type=jnp.float32)
    shape = (rows, QUARTERS * span)
    quarter = sum((iota(shape, 0) >= q * capacity).astype(jnp.int32) for q in range(1, QUARTERS))
    selector = jnp.where(quarter == iota(shape, 1) // span, hit, 0.0).astype(jnp.bfloat16)
    selector = jnp.concatenate([selector] * 3, axis=1)
    copies[0].wait()
    copies[1].wait()
    wide = out.shape[1]
    for k in range(0, wide, STEP):
        both = [both_ref[:, q * wide + k : q * wide + k + STEP] for q in range(QUARTERS)]
        out[:, k : k + STEP] = bf16_dot(selector, thirds(jnp.concatenate(both, axis=0)))
    for copy in copies[2:]:
        copy.wait()


def picked(distance, passed, chips, capacity, stored, slot, other, *after):
    slots, columns = other.shape
    block, *parts = pl.pallas_call(
        lambda *refs: pick_kernel(distance, passed, chips, capacity, *refs),
        out_shape=(float_array(QUARTERS * capacity, columns // QUARTERS),) + (float_array(slots, columns),) * len(passed),
        in_specs=[HBM, VMEM] + [ANY] * (1 + len(after)),
        out_specs=(VMEM,) * (1 + len(passed)),
        scratch_shapes=[
            pltpu.VMEM((CORES * slots, columns), jnp.float32),
            pltpu.SemaphoreType.DMA((2 + len(passed),)),
        ],
        compiler_params=BIG,
    )(stored, slot, other, *after)
    return block, [swap(part) for part in parts]


def swap(part):
    return lax.ppermute(part, "store", [(i, i ^ 1) for i in range(lax.axis_size("store"))])


def send(block, d):
    store = lax.axis_size("store")
    return lax.ppermute(block, "store", [(i, (i + d * CORES) % store) for i in range(store)])


def ordered(parts, selector):
    return bf16_dot(selector, thirds(jnp.concatenate(parts, axis=0)))


def order_kernel(*refs):
    block_refs, selector_ref, out_ref = refs[:-2], refs[-2], refs[-1]
    selector = selector_ref[...]
    for k in range(0, out_ref.shape[1], STEP):
        out_ref[:, k : k + STEP] = ordered([ref[:, k : k + STEP] for ref in block_refs], selector)


def gram_kernel(first_ref, second_ref, selector_ref, ready_ref, panel_ref, out_ref, held_ref, panel_held, sum_ref, sems):
    n, columns = panel_ref.shape
    wide = columns // QUARTERS
    fetches = []
    for k in range(0, wide, STEP):
        for i, ref in enumerate((first_ref, second_ref)):
            part = pl.ds(k, STEP)
            fetches.append(pltpu.make_async_copy(ref.at[:, part], held_ref.at[i, :, part], sems.at[0, len(fetches)]))
    for fetch in fetches:
        fetch.start()
    selector = selector_ref[...]
    top = jnp.zeros((n, STEP), jnp.float32)
    for i, k in enumerate(range(0, wide, STEP)):
        fetches[2 * i].wait()
        fetches[2 * i + 1].wait()
        got = ordered([held_ref[0, :, k : k + STEP], held_ref[1, :, k : k + STEP]], selector) + ready_ref[:, k : k + STEP]
        for q in range(QUARTERS):
            rows = got[q * n : (q + 1) * n]
            panel_held[:, q * wide + k : q * wide + k + STEP] = rows
            top = jnp.maximum(top, jnp.abs(rows))
    copies = []
    for q in range(QUARTERS):
        part = pl.ds(q * wide, wide)
        copies.append(pltpu.make_async_copy(panel_held.at[:, part], panel_ref.at[:, part], sems.at[1, q]))
        copies[-1].start()
    c, inverse = power_above(jnp.max(top, axis=1, keepdims=True))
    sum_ref[...] = jnp.zeros_like(sum_ref)

    def step(k, carry):
        block = panel_held[:, pl.ds(pl.multiple_of(k * STEP, STEP), STEP)]
        parts, _ = pieces(block * inverse, 4)
        x = jnp.concatenate([p.astype(jnp.bfloat16) for p in parts], axis=0)
        h = lax.dot_general(x[: 2 * n], x, (((1,), (1,)), ((), ())), preferred_element_type=jnp.float32)
        sum_ref[...] += h.astype(jnp.int32)
        return carry

    lax.fori_loop(0, columns // STEP, step, 0, unroll=8)
    packed = pack(*combine(sum_ref[...], c))
    for i in range(out_ref.shape[0]):
        out_ref[i] = packed
    for copy in copies:
        copy.wait()


def pack(hi, lo):
    h = hi.shape[0] // 2
    rows, columns = iota((h, h), 0), iota((h, h), 1)
    wide, diagonals = [], []
    for x in (hi, lo):
        a, b, c = x[:h, :h], x[:h, h:], x[h:, h:]
        diagonal = jnp.sum(jnp.where(rows == columns, c, 0.0), axis=0, keepdims=True)
        wide += [jnp.where(columns >= rows, a, c), b]
        diagonals += [diagonal, jnp.zeros_like(diagonal)]
    tail = jnp.broadcast_to(jnp.concatenate(diagonals, axis=1), (8, 4 * h))
    return jnp.concatenate([jnp.concatenate(wide, axis=1), tail], axis=0)


def unpack(packed):
    h = packed.shape[1] // 4
    rows, columns = iota((h, h), 0), iota((h, h), 1)
    main = packed[:h]
    turned = main.T
    out = []
    for i in (0, 2 * h):
        m, mt = main[:, i : i + h], turned[i : i + h]
        b, bt = main[:, i + h : i + 2 * h], turned[i + h : i + 2 * h]
        a = jnp.where(columns >= rows, m, mt)
        c = jnp.where(columns < rows, m, jnp.where(columns > rows, mt, packed[h : h + 1, i : i + h]))
        out.append(jnp.concatenate([jnp.concatenate([a, b], axis=1), jnp.concatenate([bt, c], axis=1)], axis=0))
    return out


def pair_sum(ref):
    lane = iota(ref.shape[1:], 1)
    half = ref.shape[2] // 2
    total, rest = ref[0], jnp.zeros(ref.shape[1:], jnp.float32)
    for i in range(1, ref.shape[0]):
        total, e = two_sum(total, ref[i])
        rest = rest + e
    rest = jnp.where(lane < half, rest * UP, 0.0)
    return total + pltpu.roll(rest, half, 1)


def sum_kernel(in_ref, out_ref):
    total = pair_sum(in_ref)
    for i in range(out_ref.shape[0]):
        out_ref[i] = total


def modes_kernel(count, pairs_ref, panel_ref, out_ref, factor_ref, panel_held, out_held, sems):
    fetch = pltpu.make_async_copy(panel_ref, panel_held, sems.at[sems.shape[0] - 1])
    fetch.start()
    weights, factor, _ = finish(*unpack(pair_sum(pairs_ref)), count)
    factor_ref[...] = factor
    n = weights.shape[0]
    w = thirds(weights)
    first, second, third = w[:n], w[n : 2 * n], w[2 * n :]
    none = jnp.zeros_like(first)
    left = jnp.concatenate(
        [
            jnp.concatenate([first, first, first], axis=1),
            jnp.concatenate([second, second, none], axis=1),
            jnp.concatenate([third, none, none], axis=1),
        ],
        axis=0,
    )
    fetch.wait()
    chunks = sems.shape[0] - 1
    wide = out_ref.shape[1] // chunks
    copies = []
    for i in range(chunks):
        for k in range(i * wide, (i + 1) * wide, STEP):
            got = bf16_dot(left, thirds(panel_held[:, k : k + STEP]))
            out_held[:, k : k + STEP] = (got[2 * n :] + got[n : 2 * n]) + got[:n]
        part = pl.ds(i * wide, wide)
        copies.append(pltpu.make_async_copy(out_held.at[:, part], out_ref.at[:, part], sems.at[i]))
        copies[-1].start()
    for copy in copies:
        copy.wait()


def float_array(*shape):
    return jax.ShapeDtypeStruct(shape, jnp.float32)


def relayout(capacity, stored, slot, other, chip, position):
    n = chip.shape[0]
    store = lax.axis_size("store")
    chips, columns = store // CORES, other.shape[1]
    z, _ = place()
    far, near = chips // 2, (1, chips - 1)
    rest = (*near, 0)
    block, others = picked(far, rest, chips, capacity, stored, slot, other)
    blocks = {far: send(block, far)}
    for d, other in zip(rest, others):
        block, _ = picked(d, (), chips, capacity, stored, slot, other, block)
        blocks[d] = send(block, d) if d else block
    distance = lax.rem(z - chip + chips, chips)
    first, last = (0, far), near

    def selector(distances):
        source = sum(jnp.where(distance == d, i + 1, 0) for i, d in enumerate(distances)) - 1
        source = jnp.where(source < 0, -(QUARTERS * capacity), source * QUARTERS * capacity + position)
        source = source[None, :] + jnp.arange(QUARTERS)[:, None] * capacity
        hit = source.reshape(-1)[:, None] == jnp.arange(len(distances) * QUARTERS * capacity)[None, :]
        return jnp.tile(hit.astype(jnp.bfloat16), (1, 3))

    ready = pl.pallas_call(
        order_kernel,
        out_shape=float_array(QUARTERS * n, columns // QUARTERS),
        compiler_params=BIG,
    )(*[blocks[d] for d in first], selector(first))
    shape = blocks[near[0]].shape
    return pl.pallas_call(
        gram_kernel,
        out_shape=(float_array(n, columns), float_array(store, n // 2 + 8, 2 * n)),
        in_specs=[ANY, ANY, VMEM, VMEM],
        out_specs=(ANY, VMEM),
        scratch_shapes=[
            pltpu.VMEM((2, *shape), jnp.float32),
            pltpu.VMEM((n, columns), jnp.float32),
            pltpu.VMEM((2 * n, 4 * n), jnp.int32),
            pltpu.SemaphoreType.DMA((2, 2 * shape[1] // STEP)),
        ],
        compiler_params=BIG,
    )(*[blocks[d] for d in last], selector(last), ready)


def per_device(stored, snap_slot):
    n = snap_slot.shape[0]
    slots = stored.shape[0]
    store, rows = lax.axis_size("store"), lax.axis_size("rows")
    columns, chips = stored.shape[1] // store, store // CORES
    part = pl.pallas_call(
        lambda *refs: part_kernel(chips // 2, chips, *refs),
        out_shape=float_array(slots, columns),
        in_specs=[HBM],
        scratch_shapes=[pltpu.SemaphoreType.DMA(())],
        compiler_params=BIG,
    )(stored)
    other = swap(part)
    chip = snap_slot // (slots * CORES)
    same = chip[:, None] == chip[None, :]
    position = jnp.sum((same & (snap_slot[None, :] < snap_slot[:, None])).astype(jnp.int32), axis=1)
    most = jnp.max(position) + 1
    capacities = (22, 24, 26, 32)
    choice = sum((most > c).astype(jnp.int32) for c in capacities[:-1])
    branches = [lambda *args, c=c: relayout(c, *args) for c in capacities]
    panel, pairs = lax.switch(choice, branches, stored, snap_slot[None, :], other, chip, position)
    pairs = lax.optimization_barrier(pairs)
    pairs = lax.all_to_all(pairs, "store", split_axis=0, concat_axis=0, tiled=True)
    pairs = pl.pallas_call(sum_kernel, out_shape=float_array(rows, *pairs.shape[1:]), compiler_params=BIG)(pairs)
    pairs = lax.all_to_all(pairs, "rows", split_axis=0, concat_axis=0, tiled=True)
    modes, factor = pl.pallas_call(
        lambda *refs: modes_kernel(columns * store * rows, *refs),
        out_shape=(float_array(n, columns), float_array(n, n)),
        in_specs=[VMEM, ANY],
        out_specs=(ANY, VMEM),
        scratch_shapes=[pltpu.VMEM((n, columns), jnp.float32)] * 2 + [pltpu.SemaphoreType.DMA((9,))],
        compiler_params=BIG,
    )(pairs, panel)
    return (modes, factor)


def solution(mesh):
    in_specs = (P("store", "rows"), P())
    out_specs = (P(None, ("rows", "store")), P())
    return jax.shard_map(
        per_device, mesh=mesh, in_specs=in_specs, out_specs=out_specs, check_vma=False
    )
```

```python
import math

import jax
import jax.numpy as jnp
from jax import lax
from jax.experimental import pallas as pl
from jax.experimental.pallas import tpu as pltpu
from jax.sharding import PartitionSpec as P

HIGHEST = lax.Precision.HIGHEST
UP = 2.0**24


def dot(a, b):
    return jnp.dot(a, b, precision=HIGHEST, preferred_element_type=jnp.float32)


def iota(shape, dim):
    return lax.broadcasted_iota(jnp.int32, shape, dim)


def power_above(value):
    c, inverse = jnp.ones_like(value), jnp.ones_like(value)
    for e in (64, 32, 16, 8, 4, 2, 1):
        big = value * inverse > 2.0**e * 0.5
        c = jnp.where(big, c * 2.0**e, c)
        inverse = jnp.where(big, inverse * 2.0**-e, inverse)
    for e in (64, 32, 16, 8, 4, 2, 1):
        small = (value * inverse <= 2.0**-e) & (c > 2.0 ** (e - 126))
        c = jnp.where(small, c * 2.0**-e, c)
        inverse = jnp.where(small, inverse * 2.0**e, inverse)
    return c, inverse


def row_of(column):
    n = column.shape[0]
    return jnp.sum(jnp.where(iota((n, n), 0) == iota((n, n), 1), column, 0.0), axis=0, keepdims=True)


def two_sum(a, b):
    s = a + b
    t = s - a
    return s, (a - (s - t)) + (b - t)


def pair_add(first, second):
    s, e = two_sum(first[0], second[0])
    return s, (first[1] + second[1]) + e * UP


def nearest(x):
    return lax.round(x, lax.RoundingMethod.TO_NEAREST_EVEN)


def pieces(x, count):
    out = []
    t = x * 256.0
    for i in range(count):
        n = nearest(t)
        out.append(n)
        t = (t - n) * 512.0
    return out, t


def levels_to_pair(levels):
    hi, lo = levels[0], jnp.zeros_like(levels[0])
    for l in range(1, len(levels)):
        hi, e = two_sum(hi, levels[l] * 2.0 ** (-9 * l))
        lo = lo + e
    return two_sum(hi, lo)


def eliminate(gram, block=8):
    n = gram.shape[0]
    rows, columns = iota((n, n), 0), iota((n, n), 1)
    whole = jnp.concatenate([gram, (rows == columns).astype(jnp.float32)], axis=1)
    lane = iota((8, 2 * n), 1)
    sub = iota((8, 2 * n), 0)
    g = n // 8
    blocks = [whole[8 * i : 8 * i + 8] for i in range(g)]
    done = []
    for b in range(g):
        cols = {}
        for i in range(b, g):
            for q in range(8):
                j = 8 * b + q
                cols[i, q] = jnp.broadcast_to(blocks[i][:, j : j + 1], (8, 2 * n))
        mult = {}
        pivots = jnp.ones((8, 2 * n), jnp.float32)
        rowsb = blocks[b]
        for q in range(8):
            pivot = jnp.broadcast_to(cols[b, q][q : q + 1], (8, 2 * n))
            pivots = jnp.where(sub == q, pivot, pivots)
            w = 1.0 / pivot
            row = jnp.broadcast_to(rowsb[q : q + 1], (8, 2 * n))
            for i in range(b, g):
                m = cols[i, q] * w
                if i == b:
                    m = jnp.where(sub > q, m, 0.0)
                mult[i, q] = m
            rowsb = rowsb - mult[b, q] * row
            for r in range(q + 1, 8):
                a = jnp.broadcast_to(cols[b, r][q : q + 1], (8, 2 * n))
                for i in range(b, g):
                    cols[i, r] = cols[i, r] - mult[i, q] * a
        for i in range(b + 1, g):
            value = blocks[i]
            for q in range(8):
                value = value - mult[i, q] * jnp.broadcast_to(rowsb[q : q + 1], (8, 2 * n))
            blocks[i] = value
        s = lax.rsqrt(pivots)
        s = s * (1.5 - 0.5 * pivots * s * s)
        done.append(rowsb * s)
    whole = jnp.concatenate(done, axis=0)
    upper = jnp.where(rows <= columns, whole[:, :n], 0.0)
    lower = jnp.where(rows >= columns, whole[:, n:], 0.0)
    return upper, lower


def bf16_dot(a, b):
    return lax.dot_general(a, b, (((1,), (0,)), ((), ())), preferred_element_type=jnp.float32)


def wide_product(left, right, keep):
    n = left[0].shape[0]
    na, nb = len(left), len(right)
    l = jnp.concatenate([x.astype(jnp.bfloat16) for x in left], axis=0)
    r = jnp.concatenate([x.astype(jnp.bfloat16) for x in right], axis=1)
    m = bf16_dot(l, r)
    out = []
    for lev in range(keep):
        acc = None
        for a in range(na):
            c = lev - a
            if 0 <= c < nb:
                t = m[a * n : (a + 1) * n, c * n : (c + 1) * n]
                acc = t if acc is None else acc + t
        out.append(acc)
    return out


def second_gram(hi, lo, lower):
    first, rest = pieces(hi, 3)
    rest = rest + lo * (2.0 ** (8 + 27) / UP)
    out = []
    for _ in range(3):
        n = nearest(rest)
        out.append(n)
        rest = (rest - n) * 512.0
    g = first + out
    top = jnp.max(jnp.abs(lower), axis=1, keepdims=True)
    u, v = power_above(top)
    ls, _ = pieces(lower * v, 4)
    lt = [x.T for x in ls]
    ur = row_of(u)
    lev = wide_product(g, lt, 7)
    ch, cl = levels_to_pair(lev)
    scale = ur * 2.0**-16
    ch, cl = ch * scale, cl * scale
    cs, rest = pieces(ch * 0.5, 3)
    rest = rest + cl * (0.5 * 2.0 ** (8 + 27))
    for _ in range(2):
        n = nearest(rest)
        cs.append(n)
        rest = (rest - n) * 512.0
    lev = wide_product(ls, cs, 7)
    h, l = levels_to_pair(lev)
    return (h + l) * (u * 2.0**-15)


def finish(hi, lo, count):
    n = hi.shape[0]
    eye = iota((n, n), 0) == iota((n, n), 1)
    diag = jnp.sum(jnp.where(eye, hi, 0.0), axis=1, keepdims=True)
    d, di = power_above(jnp.sqrt(diag))
    dr, dir_ = row_of(d), row_of(di)
    hs = (hi * di) * dir_
    ls = (lo * di) * dir_
    r1, l1 = eliminate(hs)
    g2 = second_gram(hs, ls, l1)
    r2, l2 = eliminate(g2)
    scale = math.sqrt(count)
    w = dot(l2, l1) * (dir_ * scale)
    factor = dot(r2, r1) * (dr * (1.0 / scale))
    return w, factor, g2


def combine(acc, c):
    n = acc.shape[0] // 2
    cr = row_of(c)
    part = [[acc[a * n : (a + 1) * n, b * n : (b + 1) * n] for b in range(4)] for a in range(2)]
    levels = [part[0][0], part[0][1] + part[1][0]]
    levels.append(part[0][2] + part[0][2].T + part[1][1])
    last = part[0][3] + part[1][2]
    levels.append(last + last.T)
    hi = jnp.zeros((n, n), jnp.float32)
    lo = jnp.zeros((n, n), jnp.float32)
    for lev, t in enumerate(levels):
        high = lax.shift_right_arithmetic(t, 14)
        low = (t - lax.shift_left(high, 14)).astype(jnp.float32) * 2.0 ** (-9 * lev)
        high = high.astype(jnp.float32) * 2.0 ** (14 - 9 * lev)
        hi, e = two_sum(hi, high)
        lo = lo + e
        hi, e = two_sum(hi, low)
        lo = lo + e
    hi, lo = two_sum(hi, lo)
    f = 2.0**-16
    return ((hi * f) * c) * cr, (((lo * (f * UP)) * c) * cr)


STEP = 256
CORES = 2
QUARTERS = 4
BIG = pltpu.CompilerParams(vmem_limit_bytes=8 * 2**20)
ANY = pl.BlockSpec(memory_space=pl.ANY)
HBM = pl.BlockSpec(memory_space=pltpu.HBM)
VMEM = pl.BlockSpec(memory_space=pltpu.VMEM)


def each(count, rolled, body, carry):
    if rolled:
        return lax.fori_loop(0, count, body, carry)
    for i in range(count):
        carry = body(i, carry)
    return carry


def columns_at(start):
    return pl.ds(start if isinstance(start, int) else pl.multiple_of(start, STEP), STEP)


def thirds(x):
    high = x.astype(jnp.bfloat16)
    rest = x - high.astype(jnp.float32)
    mid = rest.astype(jnp.bfloat16)
    low = (rest - mid.astype(jnp.float32)).astype(jnp.bfloat16)
    return jnp.concatenate([high, mid, low], axis=0)


def place():
    store = lax.axis_index("store")
    return store // CORES, store % CORES


def row_sum(mask_value):
    return jnp.sum(mask_value, axis=0, keepdims=True)


def positions(slot, span):
    n = slot.shape[1]
    column = jnp.sum(jnp.where(iota((n, n), 0) == iota((n, n), 1), slot, 0), axis=1, keepdims=True)
    before = (column < slot) & (column // span == slot // span)
    return slot // span, row_sum(before.astype(jnp.int32))


def part_kernel(distance, chips, stored_ref, out_ref, sem):
    columns = out_ref.shape[1]
    z, core = place()
    owner = lax.rem(z + distance, chips) * CORES + 1 - core
    start = pl.multiple_of(owner * columns, columns)
    copy = pltpu.make_async_copy(stored_ref.at[:, pl.ds(start, columns)], out_ref, sem)
    copy.start()
    copy.wait()


def pick_kernel(distance, passed, chips, capacity, stored_ref, slot_ref, other_ref, *refs):
    out, part_refs, both_ref, sems = refs[-3 - len(passed)], refs[-2 - len(passed) : -2], refs[-2], refs[-1]
    slots, columns = other_ref.shape
    z, core = place()

    def part(d, c):
        owner = lax.rem(z + d, chips) * CORES + c
        return stored_ref.at[:, pl.ds(pl.multiple_of(owner * columns, columns), columns)]

    copies = [
        pltpu.make_async_copy(part(distance, core), both_ref.at[pl.ds(0, slots)], sems.at[0]),
        pltpu.make_async_copy(other_ref, both_ref.at[pl.ds(slots, slots)], sems.at[1]),
    ]
    for i, d in enumerate(passed):
        copies.append(pltpu.make_async_copy(part(d, 1 - core), part_refs[i], sems.at[2 + i]))
    for copy in copies:
        copy.start()
    slot = slot_ref[...]
    span = CORES * slots
    chip, position = positions(slot, span)
    local = slot - (chip * CORES + core) * slots
    local = jnp.where(local < 0, local + span, local)
    count = slot.shape[1]
    rows = QUARTERS * capacity
    row, column = iota((rows, count), 0), iota((span, count), 0)
    quarter = sum((row >= q * capacity).astype(jnp.int32) for q in range(1, QUARTERS))
    ranks = ((chip == z) & (position == row - quarter * capacity)).astype(jnp.bfloat16)
    locals_ = (local == column).astype(jnp.bfloat16)
    locals_ = jnp.concatenate([locals_] * QUARTERS, axis=0)
    hit = lax.dot_general(ranks, locals_, (((1,), (1,)), ((), ())), preferred_element_type=jnp.float32)
    shape = (rows, QUARTERS * span)
    quarter = sum((iota(shape, 0) >= q * capacity).astype(jnp.int32) for q in range(1, QUARTERS))
    selector = jnp.where(quarter == iota(shape, 1) // span, hit, 0.0).astype(jnp.bfloat16)
    selector = jnp.concatenate([selector] * 3, axis=1)
    copies[0].wait()
    copies[1].wait()
    wide = out.shape[1]

    def step(i, carry):
        both = [both_ref[:, columns_at(q * wide + i * STEP)] for q in range(QUARTERS)]
        out[:, columns_at(i * STEP)] = bf16_dot(selector, thirds(jnp.concatenate(both, axis=0)))
        return carry

    each(wide // STEP, not passed, step, 0)
    for copy in copies[2:]:
        copy.wait()


def picked(distance, passed, chips, capacity, stored, slot, other, *after):
    slots, columns = other.shape
    block, *parts = pl.pallas_call(
        lambda *refs: pick_kernel(distance, passed, chips, capacity, *refs),
        out_shape=(float_array(QUARTERS * capacity, columns // QUARTERS),) + (float_array(slots, columns),) * len(passed),
        in_specs=[HBM, VMEM] + [ANY] * (1 + len(after)),
        out_specs=(VMEM,) * (1 + len(passed)),
        scratch_shapes=[
            pltpu.VMEM((CORES * slots, columns), jnp.float32),
            pltpu.SemaphoreType.DMA((2 + len(passed),)),
        ],
        compiler_params=BIG,
    )(stored, slot, other, *after)
    return block, [swap(part) for part in parts]


def swap(part):
    return lax.ppermute(part, "store", [(i, i ^ 1) for i in range(lax.axis_size("store"))])


def send(block, d):
    store = lax.axis_size("store")
    return lax.ppermute(block, "store", [(i, (i + d * CORES) % store) for i in range(store)])


def ordered(parts, selector):
    return bf16_dot(selector, thirds(jnp.concatenate(parts, axis=0)))


def order_kernel(*refs):
    block_refs, selector_ref, out_ref = refs[:-2], refs[-2], refs[-1]
    selector = selector_ref[...]

    def step(i, carry):
        part = columns_at(i * STEP)
        out_ref[:, part] = ordered([ref[:, part] for ref in block_refs], selector)
        return carry

    each(out_ref.shape[1] // STEP, True, step, 0)


def gram_kernel(rolled, *refs):
    first_ref, second_ref, selector_ref, ready_ref, panel_ref, out_ref, held_ref, panel_held, sum_ref, sems = refs
    n, columns = panel_ref.shape
    wide = columns // QUARTERS

    fetches = []
    for j, ref in enumerate((first_ref, second_ref)):
        fetches.append(pltpu.make_async_copy(ref, held_ref.at[j], sems.at[0, j]))
        fetches[-1].start()
    selector = selector_ref[...]

    for fetch in fetches:
        fetch.wait()

    def gather(i, top):
        part = columns_at(i * STEP)
        got = ordered([held_ref[0, :, part], held_ref[1, :, part]], selector) + ready_ref[:, part]
        for q in range(QUARTERS):
            rows = got[q * n : (q + 1) * n]
            panel_held[:, columns_at(q * wide + i * STEP)] = rows
            top = jnp.maximum(top, jnp.abs(rows))
        return top

    top = each(wide // STEP, rolled, gather, jnp.zeros((n, STEP), jnp.float32))
    copies = []
    for q in range(QUARTERS):
        part = pl.ds(q * wide, wide)
        copies.append(pltpu.make_async_copy(panel_held.at[:, part], panel_ref.at[:, part], sems.at[1, q]))
        copies[-1].start()
    c, inverse = power_above(jnp.max(top, axis=1, keepdims=True))
    sum_ref[...] = jnp.zeros_like(sum_ref)

    def step(i, carry):
        parts, _ = pieces(panel_held[:, columns_at(i * STEP)] * inverse, 4)
        x = jnp.concatenate([p.astype(jnp.bfloat16) for p in parts], axis=0)
        h = lax.dot_general(x[: 2 * n], x, (((1,), (1,)), ((), ())), preferred_element_type=jnp.float32)
        sum_ref[...] += h.astype(jnp.int32)
        return carry

    each(columns // STEP, rolled, step, 0)
    packed = pack(*combine(sum_ref[...], c))
    for i in range(out_ref.shape[0]):
        out_ref[i] = packed
    for copy in copies:
        copy.wait()


def pack(hi, lo):
    h = hi.shape[0] // 2
    rows, columns = iota((h, h), 0), iota((h, h), 1)
    wide, diagonals = [], []
    for x in (hi, lo):
        a, b, c = x[:h, :h], x[:h, h:], x[h:, h:]
        diagonal = jnp.sum(jnp.where(rows == columns, c, 0.0), axis=0, keepdims=True)
        wide += [jnp.where(columns >= rows, a, c), b]
        diagonals += [diagonal, jnp.zeros_like(diagonal)]
    tail = jnp.broadcast_to(jnp.concatenate(diagonals, axis=1), (8, 4 * h))
    return jnp.concatenate([jnp.concatenate(wide, axis=1), tail], axis=0)


def unpack(packed):
    h = packed.shape[1] // 4
    rows, columns = iota((h, h), 0), iota((h, h), 1)
    main = packed[:h]
    turned = main.T
    out = []
    for i in (0, 2 * h):
        m, mt = main[:, i : i + h], turned[i : i + h]
        b, bt = main[:, i + h : i + 2 * h], turned[i + h : i + 2 * h]
        a = jnp.where(columns >= rows, m, mt)
        c = jnp.where(columns < rows, m, jnp.where(columns > rows, mt, packed[h : h + 1, i : i + h]))
        out.append(jnp.concatenate([jnp.concatenate([a, b], axis=1), jnp.concatenate([bt, c], axis=1)], axis=0))
    return out


def pair_sum(ref):
    lane = iota(ref.shape[1:], 1)
    half = ref.shape[2] // 2
    total, rest = ref[0], jnp.zeros(ref.shape[1:], jnp.float32)
    for i in range(1, ref.shape[0]):
        total, e = two_sum(total, ref[i])
        rest = rest + e
    rest = jnp.where(lane < half, rest * UP, 0.0)
    return total + pltpu.roll(rest, half, 1)


def sum_kernel(in_ref, out_ref):
    total = pair_sum(in_ref)
    for i in range(out_ref.shape[0]):
        out_ref[i] = total


def modes_kernel(count, pairs_ref, panel_ref, out_ref, factor_ref, panel_held, out_held, sems):
    fetch = pltpu.make_async_copy(panel_ref, panel_held, sems.at[sems.shape[0] - 1])
    fetch.start()
    weights, factor, _ = finish(*unpack(pair_sum(pairs_ref)), count)
    factor_ref[...] = factor
    n = weights.shape[0]
    w = thirds(weights)
    first, second, third = w[:n], w[n : 2 * n], w[2 * n :]
    none = jnp.zeros_like(first)
    left = jnp.concatenate(
        [
            jnp.concatenate([first, first, first], axis=1),
            jnp.concatenate([second, second, none], axis=1),
            jnp.concatenate([third, none, none], axis=1),
        ],
        axis=0,
    )
    fetch.wait()
    chunks = sems.shape[0] - 1
    wide = out_ref.shape[1] // chunks
    copies = []
    for i in range(chunks):
        for k in range(i * wide, (i + 1) * wide, STEP):
            got = bf16_dot(left, thirds(panel_held[:, k : k + STEP]))
            out_held[:, k : k + STEP] = (got[2 * n :] + got[n : 2 * n]) + got[:n]
        part = pl.ds(i * wide, wide)
        copies.append(pltpu.make_async_copy(out_held.at[:, part], out_ref.at[:, part], sems.at[i]))
        copies[-1].start()
    for copy in copies:
        copy.wait()


def float_array(*shape):
    return jax.ShapeDtypeStruct(shape, jnp.float32)


def relayout(capacity, stored, slot, other, chip, position):
    n = chip.shape[0]
    store = lax.axis_size("store")
    chips, columns = store // CORES, other.shape[1]
    z, _ = place()
    far, near = chips // 2, (1, chips - 1)
    rest = (*near, 0)
    block, others = picked(far, rest, chips, capacity, stored, slot, other)
    blocks = {far: send(block, far)}
    for d, other in zip(rest, others):
        block, _ = picked(d, (), chips, capacity, stored, slot, other, block)
        blocks[d] = send(block, d) if d else block
    distance = lax.rem(z - chip + chips, chips)
    first, last = (0, far), near

    def selector(distances):
        source = sum(jnp.where(distance == d, i + 1, 0) for i, d in enumerate(distances)) - 1
        source = jnp.where(source < 0, -(QUARTERS * capacity), source * QUARTERS * capacity + position)
        source = source[None, :] + jnp.arange(QUARTERS)[:, None] * capacity
        hit = source.reshape(-1)[:, None] == jnp.arange(len(distances) * QUARTERS * capacity)[None, :]
        return jnp.tile(hit.astype(jnp.bfloat16), (1, 3))

    ready = pl.pallas_call(
        order_kernel,
        out_shape=float_array(QUARTERS * n, columns // QUARTERS),
        compiler_params=BIG,
    )(*[blocks[d] for d in first], selector(first))
    shape = blocks[near[0]].shape
    return pl.pallas_call(
        lambda *refs: gram_kernel(capacity == CORES * stored.shape[0], *refs),
        out_shape=(float_array(n, columns), float_array(store, n // 2 + 8, 2 * n)),
        in_specs=[ANY, ANY, VMEM, VMEM],
        out_specs=(ANY, VMEM),
        scratch_shapes=[
            pltpu.VMEM((2, *shape), jnp.float32),
            pltpu.VMEM((n, columns), jnp.float32),
            pltpu.VMEM((2 * n, 4 * n), jnp.int32),
            pltpu.SemaphoreType.DMA((2, QUARTERS)),
        ],
        compiler_params=BIG,
    )(*[blocks[d] for d in last], selector(last), ready)


def per_device(stored, snap_slot):
    n = snap_slot.shape[0]
    slots = stored.shape[0]
    store, rows = lax.axis_size("store"), lax.axis_size("rows")
    columns, chips = stored.shape[1] // store, store // CORES
    part = pl.pallas_call(
        lambda *refs: part_kernel(chips // 2, chips, *refs),
        out_shape=float_array(slots, columns),
        in_specs=[HBM],
        scratch_shapes=[pltpu.SemaphoreType.DMA(())],
        compiler_params=BIG,
    )(stored)
    other = swap(part)
    chip = snap_slot // (slots * CORES)
    same = chip[:, None] == chip[None, :]
    position = jnp.sum((same & (snap_slot[None, :] < snap_slot[:, None])).astype(jnp.int32), axis=1)
    most = jnp.max(position) + 1
    capacities = (22, 24, 26, 32)
    choice = sum((most > c).astype(jnp.int32) for c in capacities[:-1])
    branches = [lambda *args, c=c: relayout(c, *args) for c in capacities]
    panel, pairs = lax.switch(choice, branches, stored, snap_slot[None, :], other, chip, position)
    pairs = lax.optimization_barrier(pairs)
    pairs = lax.all_to_all(pairs, "store", split_axis=0, concat_axis=0, tiled=True)
    pairs = pl.pallas_call(sum_kernel, out_shape=float_array(rows, *pairs.shape[1:]), compiler_params=BIG)(pairs)
    pairs = lax.all_to_all(pairs, "rows", split_axis=0, concat_axis=0, tiled=True)
    modes, factor = pl.pallas_call(
        lambda *refs: modes_kernel(columns * store * rows, *refs),
        out_shape=(float_array(n, columns), float_array(n, n)),
        in_specs=[VMEM, ANY],
        out_specs=(ANY, VMEM),
        scratch_shapes=[pltpu.VMEM((n, columns), jnp.float32)] * 2 + [pltpu.SemaphoreType.DMA((9,))],
        compiler_params=BIG,
    )(pairs, panel)
    return (modes, factor)


def solution(mesh):
    in_specs = (P("store", "rows"), P())
    out_specs = (P(None, ("rows", "store")), P())
    return jax.shard_map(
        per_device, mesh=mesh, in_specs=in_specs, out_specs=out_specs, check_vma=False
    )
```

```python
import math

import jax
import jax.numpy as jnp
from jax import lax
from jax.experimental import pallas as pl
from jax.experimental.pallas import tpu as pltpu
from jax.sharding import PartitionSpec as P

HIGHEST = lax.Precision.HIGHEST
UP = 2.0**24


def dot(a, b):
    return jnp.dot(a, b, precision=HIGHEST, preferred_element_type=jnp.float32)


def iota(shape, dim):
    return lax.broadcasted_iota(jnp.int32, shape, dim)


def power_above(value):
    c, inverse = jnp.ones_like(value), jnp.ones_like(value)
    for e in (64, 32, 16, 8, 4, 2, 1):
        big = value * inverse > 2.0**e * 0.5
        c = jnp.where(big, c * 2.0**e, c)
        inverse = jnp.where(big, inverse * 2.0**-e, inverse)
    for e in (64, 32, 16, 8, 4, 2, 1):
        small = (value * inverse <= 2.0**-e) & (c > 2.0 ** (e - 126))
        c = jnp.where(small, c * 2.0**-e, c)
        inverse = jnp.where(small, inverse * 2.0**e, inverse)
    return c, inverse


def row_of(column):
    n = column.shape[0]
    return jnp.sum(jnp.where(iota((n, n), 0) == iota((n, n), 1), column, 0.0), axis=0, keepdims=True)


def two_sum(a, b):
    s = a + b
    t = s - a
    return s, (a - (s - t)) + (b - t)


def pair_add(first, second):
    s, e = two_sum(first[0], second[0])
    return s, (first[1] + second[1]) + e * UP


def nearest(x):
    return lax.round(x, lax.RoundingMethod.TO_NEAREST_EVEN)


def pieces(x, count):
    out = []
    t = x * 256.0
    for i in range(count):
        n = nearest(t)
        out.append(n)
        t = (t - n) * 512.0
    return out, t


def levels_to_pair(levels):
    hi, lo = levels[0], jnp.zeros_like(levels[0])
    for l in range(1, len(levels)):
        hi, e = two_sum(hi, levels[l] * 2.0 ** (-9 * l))
        lo = lo + e
    return two_sum(hi, lo)


def eliminate(gram, block=8):
    n = gram.shape[0]
    rows, columns = iota((n, n), 0), iota((n, n), 1)
    whole = jnp.concatenate([gram, (rows == columns).astype(jnp.float32)], axis=1)
    lane = iota((8, 2 * n), 1)
    sub = iota((8, 2 * n), 0)
    g = n // 8
    blocks = [whole[8 * i : 8 * i + 8] for i in range(g)]
    done = []
    for b in range(g):
        cols = {}
        for i in range(b, g):
            for q in range(8):
                j = 8 * b + q
                cols[i, q] = jnp.broadcast_to(blocks[i][:, j : j + 1], (8, 2 * n))
        mult = {}
        pivots = jnp.ones((8, 2 * n), jnp.float32)
        rowsb = blocks[b]

        def spread(value, q):
            return jnp.broadcast_to(value[q : q + 1], (8, 2 * n))

        for q in range(0, 8, 2):
            p, o, r = spread(cols[b, q], q), spread(cols[b, q + 1], q), spread(cols[b, q + 1], q + 1)
            determinant = p * r - o * o
            w, v = 1.0 / p, p * (1.0 / determinant)
            ratio = o * w
            for i in range(b, g):
                first = cols[i, q] * w
                second = (cols[i, q + 1] - cols[i, q] * ratio) * v
                if i == b:
                    first = jnp.where(sub > q, first, 0.0)
                    second = jnp.where(sub > q + 1, second, 0.0)
                mult[i, q], mult[i, q + 1] = first, second
            pivots = jnp.where(sub == q, p, jnp.where(sub == q + 1, r - o * ratio, pivots))
            row = spread(rowsb, q)
            rowsb = rowsb - mult[b, q] * row
            rowsb = rowsb - mult[b, q + 1] * spread(rowsb, q + 1)
            for c in range(q + 2, 8):
                a0 = spread(cols[b, c], q)
                a1 = spread(cols[b, c], q + 1) - ratio * a0
                for i in range(b, g):
                    cols[i, c] = (cols[i, c] - mult[i, q] * a0) - mult[i, q + 1] * a1
        for i in range(b + 1, g):
            value = blocks[i]
            for q in range(8):
                value = value - mult[i, q] * jnp.broadcast_to(rowsb[q : q + 1], (8, 2 * n))
            blocks[i] = value
        s = lax.rsqrt(pivots)
        s = s * (1.5 - 0.5 * pivots * s * s)
        done.append(rowsb * s)
    whole = jnp.concatenate(done, axis=0)
    upper = jnp.where(rows <= columns, whole[:, :n], 0.0)
    lower = jnp.where(rows >= columns, whole[:, n:], 0.0)
    return upper, lower


def bf16_dot(a, b):
    return lax.dot_general(a, b, (((1,), (0,)), ((), ())), preferred_element_type=jnp.float32)


def wide_product(left, right, keep):
    n = left[0].shape[0]
    na, nb = len(left), len(right)
    l = jnp.concatenate([x.astype(jnp.bfloat16) for x in left], axis=0)
    r = jnp.concatenate([x.astype(jnp.bfloat16) for x in right], axis=1)
    m = bf16_dot(l, r)
    out = []
    for lev in range(keep):
        acc = None
        for a in range(na):
            c = lev - a
            if 0 <= c < nb:
                t = m[a * n : (a + 1) * n, c * n : (c + 1) * n]
                acc = t if acc is None else acc + t
        out.append(acc)
    return out


def second_gram(hi, lo, lower):
    first, rest = pieces(hi, 3)
    rest = rest + lo * (2.0 ** (8 + 27) / UP)
    out = []
    for _ in range(3):
        n = nearest(rest)
        out.append(n)
        rest = (rest - n) * 512.0
    g = first + out
    top = jnp.max(jnp.abs(lower), axis=1, keepdims=True)
    u, v = power_above(top)
    ls, _ = pieces(lower * v, 4)
    lt = [x.T for x in ls]
    ur = row_of(u)
    lev = wide_product(g, lt, 7)
    ch, cl = levels_to_pair(lev)
    scale = ur * 2.0**-16
    ch, cl = ch * scale, cl * scale
    cs, rest = pieces(ch * 0.5, 3)
    rest = rest + cl * (0.5 * 2.0 ** (8 + 27))
    for _ in range(2):
        n = nearest(rest)
        cs.append(n)
        rest = (rest - n) * 512.0
    lev = wide_product(ls, cs, 7)
    h, l = levels_to_pair(lev)
    return (h + l) * (u * 2.0**-15)


def finish(hi, lo, count):
    n = hi.shape[0]
    eye = iota((n, n), 0) == iota((n, n), 1)
    diag = jnp.sum(jnp.where(eye, hi, 0.0), axis=1, keepdims=True)
    d, di = power_above(jnp.sqrt(diag))
    dr, dir_ = row_of(d), row_of(di)
    hs = (hi * di) * dir_
    ls = (lo * di) * dir_
    r1, l1 = eliminate(hs)
    g2 = second_gram(hs, ls, l1)
    r2, l2 = eliminate(g2)
    scale = math.sqrt(count)
    w = dot(l2, l1) * (dir_ * scale)
    factor = dot(r2, r1) * (dr * (1.0 / scale))
    return w, factor, g2


def combine(acc, c):
    n = acc.shape[0] // 3
    cr = row_of(c)
    part = [[acc[a * n : (a + 1) * n, b * n : (b + 1) * n] for b in range(4)] for a in range(3)]
    levels = []
    for lev in range(6):
        total = None
        for a in range(3):
            b = lev - a
            if 0 <= b < 4:
                x = part[a][b] + part[a][b].T if b == 3 else part[a][b]
                total = x if total is None else total + x
        levels.append(total)
    hi = jnp.zeros((n, n), jnp.float32)
    lo = jnp.zeros((n, n), jnp.float32)
    for lev, t in enumerate(levels):
        high = lax.shift_right_arithmetic(t, 14)
        low = (t - lax.shift_left(high, 14)).astype(jnp.float32) * 2.0 ** (-9 * lev)
        high = high.astype(jnp.float32) * 2.0 ** (14 - 9 * lev)
        hi, e = two_sum(hi, high)
        lo = lo + e
        hi, e = two_sum(hi, low)
        lo = lo + e
    hi, lo = two_sum(hi, lo)
    f = 2.0**-16
    return ((hi * f) * c) * cr, (((lo * (f * UP)) * c) * cr)


STEP = 256
CORES = 2
QUARTERS = 4
BIG = pltpu.CompilerParams(vmem_limit_bytes=8 * 2**20)
ANY = pl.BlockSpec(memory_space=pl.ANY)
HBM = pl.BlockSpec(memory_space=pltpu.HBM)
VMEM = pl.BlockSpec(memory_space=pltpu.VMEM)


def each(count, rolled, body, carry):
    if rolled:
        return lax.fori_loop(0, count, body, carry)
    for i in range(count):
        carry = body(i, carry)
    return carry


def columns_at(start):
    return pl.ds(start if isinstance(start, int) else pl.multiple_of(start, STEP), STEP)


def thirds(x):
    high = x.astype(jnp.bfloat16)
    rest = x - high.astype(jnp.float32)
    mid = rest.astype(jnp.bfloat16)
    low = (rest - mid.astype(jnp.float32)).astype(jnp.bfloat16)
    return jnp.concatenate([high, mid, low], axis=0)


def place():
    store = lax.axis_index("store")
    return store // CORES, store % CORES


def row_sum(mask_value):
    return jnp.sum(mask_value, axis=0, keepdims=True)


def positions(slot, span):
    n = slot.shape[1]
    column = jnp.sum(jnp.where(iota((n, n), 0) == iota((n, n), 1), slot, 0), axis=1, keepdims=True)
    before = (column < slot) & (column // span == slot // span)
    return slot // span, row_sum(before.astype(jnp.int32))


def part_kernel(distance, chips, stored_ref, out_ref, sem):
    columns = out_ref.shape[1]
    z, core = place()
    owner = lax.rem(z + distance, chips) * CORES + 1 - core
    start = pl.multiple_of(owner * columns, columns)
    copy = pltpu.make_async_copy(stored_ref.at[:, pl.ds(start, columns)], out_ref, sem)
    copy.start()
    copy.wait()


def pick_kernel(distance, passed, index, chips, capacity, *refs):
    stored_ref, slot_ref, other_ref = refs[:3]
    sems = refs[-1]
    slots, columns = other_ref.shape[-2:]
    z, core = place()

    def part(d, c):
        owner = lax.rem(z + d, chips) * CORES + c
        return stored_ref.at[:, pl.ds(pl.multiple_of(owner * columns, columns), columns)]

    copies = []
    if passed:
        out, parts_ref, own_ref, held_ref = refs[-5:-1]
        copies.append(pltpu.make_async_copy(part(distance, core), own_ref, sems.at[0]))
        for i, d in enumerate(passed):
            copies.append(pltpu.make_async_copy(part(d, 1 - core), held_ref.at[i], sems.at[1 + i]))
    else:
        out, own_ref, got_ref = refs[-4:-1]
        copies.append(pltpu.make_async_copy(part(distance, core), own_ref, sems.at[0]))
        copies.append(pltpu.make_async_copy(other_ref.at[index], got_ref, sems.at[1]))
        other_ref = got_ref
    for copy in copies:
        copy.start()
    slot = slot_ref[...]
    span = CORES * slots
    chip, position = positions(slot, span)
    local = slot - (chip * CORES + core) * slots
    local = jnp.where(local < 0, local + span, local)
    count = slot.shape[1]
    rows = QUARTERS * capacity
    row, column = iota((rows, count), 0), iota((span, count), 0)
    quarter = sum((row >= q * capacity).astype(jnp.int32) for q in range(1, QUARTERS))
    ranks = ((chip == z) & (position == row - quarter * capacity)).astype(jnp.bfloat16)
    locals_ = (local == column).astype(jnp.bfloat16)
    locals_ = jnp.concatenate([locals_] * QUARTERS, axis=0)
    hit = lax.dot_general(ranks, locals_, (((1,), (1,)), ((), ())), preferred_element_type=jnp.float32)
    shape = (rows, QUARTERS * span)
    quarter = sum((iota(shape, 0) >= q * capacity).astype(jnp.int32) for q in range(1, QUARTERS))
    selector = jnp.where(quarter == iota(shape, 1) // span, hit, 0.0).astype(jnp.bfloat16)
    selector = jnp.concatenate([selector] * 3, axis=1)
    wide = out.shape[1]

    def step(i, carry):
        at = [columns_at(q * wide + i * STEP) for q in range(QUARTERS)]
        both = [ref[:, part] for part in at for ref in (own_ref, other_ref)]
        out[:, columns_at(i * STEP)] = bf16_dot(selector, thirds(jnp.concatenate(both, axis=0)))
        return carry

    if not passed:
        for copy in copies:
            copy.wait()
        each(wide // STEP, True, step, 0)
        return
    copies[0].wait()
    half = wide // STEP // 2
    each(half, False, step, 0)
    ends = []
    for i in range(len(passed)):
        copies[1 + i].wait()
        ends.append(pltpu.make_async_copy(held_ref.at[i], parts_ref.at[i], sems.at[1 + i]))
        ends[-1].start()
    each(wide // STEP - half, False, lambda i, carry: step(half + i, carry), 0)
    for end in ends:
        end.wait()


def picked(distance, chips, capacity, stored, slot, others, index, *after):
    _, slots, columns = others.shape
    return pl.pallas_call(
        lambda *refs: pick_kernel(distance, (), index, chips, capacity, *refs),
        out_shape=float_array(QUARTERS * capacity, columns // QUARTERS),
        in_specs=[HBM, VMEM, ANY] + [ANY] * len(after),
        scratch_shapes=[pltpu.VMEM((slots, columns), jnp.float32)] * 2 + [pltpu.SemaphoreType.DMA((2,))],
        compiler_params=BIG,
    )(stored, slot, others, *after)


def picked_first(distance, passed, chips, capacity, stored, slot, other):
    slots, columns = other.shape
    count = len(passed)
    return pl.pallas_call(
        lambda *refs: pick_kernel(distance, passed, None, chips, capacity, *refs),
        out_shape=(float_array(QUARTERS * capacity, columns // QUARTERS), float_array(count, slots, columns)),
        in_specs=[HBM, VMEM, VMEM],
        out_specs=(VMEM, ANY),
        scratch_shapes=[
            pltpu.VMEM((slots, columns), jnp.float32),
            pltpu.VMEM((count, slots, columns), jnp.float32),
            pltpu.SemaphoreType.DMA((1 + count,)),
        ],
        compiler_params=BIG,
    )(stored, slot, other)


def swap(part):
    return lax.ppermute(part, "store", [(i, i ^ 1) for i in range(lax.axis_size("store"))])


def send(block, d):
    store = lax.axis_size("store")
    return lax.ppermute(block, "store", [(i, (i + d * CORES) % store) for i in range(store)])


def ordered(parts, selector):
    return bf16_dot(selector, thirds(jnp.concatenate(parts, axis=0)))


def order_kernel(*refs):
    block_refs, selector_ref, out_ref = refs[:-2], refs[-2], refs[-1]
    selector = selector_ref[...]

    def step(i, carry):
        part = columns_at(i * STEP)
        out_ref[:, part] = ordered([ref[:, part] for ref in block_refs], selector)
        return carry

    each(out_ref.shape[1] // STEP, True, step, 0)


def gram_kernel(rolled, *refs):
    first_ref, second_ref, selector_ref, ready_ref, panel_ref, out_ref, held_ref, panel_held, sum_ref, sems = refs
    n, columns = panel_ref.shape
    wide = columns // QUARTERS

    fetches = []
    for j, ref in enumerate((first_ref, second_ref)):
        fetches.append(pltpu.make_async_copy(ref, held_ref.at[j], sems.at[0, j]))
        fetches[-1].start()
    selector = selector_ref[...]

    for fetch in fetches:
        fetch.wait()

    def gather(i, top):
        part = columns_at(i * STEP)
        got = ordered([held_ref[0, :, part], held_ref[1, :, part]], selector) + ready_ref[:, part]
        for q in range(QUARTERS):
            rows = got[q * n : (q + 1) * n]
            panel_held[:, columns_at(q * wide + i * STEP)] = rows
            top = jnp.maximum(top, jnp.abs(rows))
        return top

    top = each(wide // STEP, rolled, gather, jnp.zeros((n, STEP), jnp.float32))
    copies = []
    for q in range(QUARTERS):
        part = pl.ds(q * wide, wide)
        copies.append(pltpu.make_async_copy(panel_held.at[:, part], panel_ref.at[:, part], sems.at[1, q]))
        copies[-1].start()
    c, inverse = power_above(jnp.max(top, axis=1, keepdims=True))
    sum_ref[...] = jnp.zeros_like(sum_ref)

    def step(i, carry):
        parts, _ = pieces(panel_held[:, columns_at(i * STEP)] * inverse, 4)
        x = jnp.concatenate([p.astype(jnp.bfloat16) for p in parts], axis=0)
        h = lax.dot_general(x[: 3 * n], x, (((1,), (1,)), ((), ())), preferred_element_type=jnp.float32)
        sum_ref[...] += h.astype(jnp.int32)
        return carry

    each(columns // STEP, rolled, step, 0)
    packed = pack(*combine(sum_ref[...], c))
    for i in range(out_ref.shape[0]):
        out_ref[i] = packed
    for copy in copies:
        copy.wait()


def pack(hi, lo):
    h = hi.shape[0] // 2
    rows, columns = iota((h, h), 0), iota((h, h), 1)
    wide, diagonals = [], []
    for x in (hi, lo):
        a, b, c = x[:h, :h], x[:h, h:], x[h:, h:]
        diagonal = jnp.sum(jnp.where(rows == columns, c, 0.0), axis=0, keepdims=True)
        wide += [jnp.where(columns >= rows, a, c), b]
        diagonals += [diagonal, jnp.zeros_like(diagonal)]
    tail = jnp.broadcast_to(jnp.concatenate(diagonals, axis=1), (8, 4 * h))
    return jnp.concatenate([jnp.concatenate(wide, axis=1), tail], axis=0)


def unpack(packed):
    h = packed.shape[1] // 4
    rows, columns = iota((h, h), 0), iota((h, h), 1)
    main = packed[:h]
    turned = main.T
    out = []
    for i in (0, 2 * h):
        m, mt = main[:, i : i + h], turned[i : i + h]
        b, bt = main[:, i + h : i + 2 * h], turned[i + h : i + 2 * h]
        a = jnp.where(columns >= rows, m, mt)
        c = jnp.where(columns < rows, m, jnp.where(columns > rows, mt, packed[h : h + 1, i : i + h]))
        out.append(jnp.concatenate([jnp.concatenate([a, b], axis=1), jnp.concatenate([bt, c], axis=1)], axis=0))
    return out


def pair_sum(ref):
    half = ref.shape[2] // 2
    terms = [(ref[i], None) for i in range(ref.shape[0])]
    while len(terms) > 1:
        merged = []
        for (x, a), (y, b) in zip(terms[::2], terms[1::2]):
            total, e = two_sum(x, y)
            merged.append((total, e if a is None else (a + b) + e))
        terms = merged
    total, rest = terms[0]
    rest = jnp.where(iota(total.shape, 1) < half, rest * UP, 0.0)
    return total + pltpu.roll(rest, half, 1)


def sum_kernel(in_ref, out_ref):
    total = pair_sum(in_ref)
    for i in range(out_ref.shape[0]):
        out_ref[i] = total


def modes_kernel(count, pairs_ref, panel_ref, out_ref, factor_ref, panel_held, out_held, sems):
    fetch = pltpu.make_async_copy(panel_ref, panel_held, sems.at[sems.shape[0] - 1])
    fetch.start()
    weights, factor, _ = finish(*unpack(pair_sum(pairs_ref)), count)
    factor_ref[...] = factor
    n = weights.shape[0]
    w = thirds(weights)
    first, second, third = w[:n], w[n : 2 * n], w[2 * n :]
    none = jnp.zeros_like(first)
    left = jnp.concatenate(
        [
            jnp.concatenate([first, first, first], axis=1),
            jnp.concatenate([second, second, none], axis=1),
            jnp.concatenate([third, none, none], axis=1),
        ],
        axis=0,
    )
    fetch.wait()
    chunks = sems.shape[0] - 1
    wide = out_ref.shape[1] // chunks
    copies = []
    for i in range(chunks):
        for k in range(i * wide, (i + 1) * wide, STEP):
            got = bf16_dot(left, thirds(panel_held[:, k : k + STEP]))
            out_held[:, k : k + STEP] = (got[2 * n :] + got[n : 2 * n]) + got[:n]
        part = pl.ds(i * wide, wide)
        copies.append(pltpu.make_async_copy(out_held.at[:, part], out_ref.at[:, part], sems.at[i]))
        copies[-1].start()
    for copy in copies:
        copy.wait()


def float_array(*shape):
    return jax.ShapeDtypeStruct(shape, jnp.float32)


def relayout(capacity, stored, slot, other, chip, position):
    n = chip.shape[0]
    store = lax.axis_size("store")
    chips, columns = store // CORES, other.shape[1]
    z, _ = place()
    far, near = chips // 2, (1, chips - 1)
    rest = (*near, 0)
    block, parts = picked_first(far, rest, chips, capacity, stored, slot, other)
    blocks = {far: send(block, far)}
    others = swap(parts)
    for i, d in enumerate(rest):
        block = picked(d, chips, capacity, stored, slot, others, i, block)
        blocks[d] = send(block, d) if d else block
    distance = lax.rem(z - chip + chips, chips)
    first, last = (0, far), near

    def selector(distances):
        source = sum(jnp.where(distance == d, i + 1, 0) for i, d in enumerate(distances)) - 1
        source = jnp.where(source < 0, -(QUARTERS * capacity), source * QUARTERS * capacity + position)
        source = source[None, :] + jnp.arange(QUARTERS)[:, None] * capacity
        hit = source.reshape(-1)[:, None] == jnp.arange(len(distances) * QUARTERS * capacity)[None, :]
        return jnp.tile(hit.astype(jnp.bfloat16), (1, 3))

    ready = pl.pallas_call(
        order_kernel,
        out_shape=float_array(QUARTERS * n, columns // QUARTERS),
        compiler_params=BIG,
    )(*[blocks[d] for d in first], selector(first))
    shape = blocks[near[0]].shape
    return pl.pallas_call(
        lambda *refs: gram_kernel(capacity == CORES * stored.shape[0], *refs),
        out_shape=(float_array(n, columns), float_array(store, n // 2 + 8, 2 * n)),
        in_specs=[ANY, ANY, VMEM, VMEM],
        out_specs=(ANY, VMEM),
        scratch_shapes=[
            pltpu.VMEM((2, *shape), jnp.float32),
            pltpu.VMEM((n, columns), jnp.float32),
            pltpu.VMEM((3 * n, 4 * n), jnp.int32),
            pltpu.SemaphoreType.DMA((2, QUARTERS)),
        ],
        compiler_params=BIG,
    )(*[blocks[d] for d in last], selector(last), ready)


def per_device(stored, snap_slot):
    n = snap_slot.shape[0]
    slots = stored.shape[0]
    store, rows = lax.axis_size("store"), lax.axis_size("rows")
    columns, chips = stored.shape[1] // store, store // CORES
    part = pl.pallas_call(
        lambda *refs: part_kernel(chips // 2, chips, *refs),
        out_shape=float_array(slots, columns),
        in_specs=[HBM],
        scratch_shapes=[pltpu.SemaphoreType.DMA(())],
        compiler_params=BIG,
    )(stored)
    other = swap(part)
    chip = snap_slot // (slots * CORES)
    same = chip[:, None] == chip[None, :]
    position = jnp.sum((same & (snap_slot[None, :] < snap_slot[:, None])).astype(jnp.int32), axis=1)
    most = jnp.max(position) + 1
    capacities = (22, 24, 26, 32)
    choice = sum((most > c).astype(jnp.int32) for c in capacities[:-1])
    branches = [lambda *args, c=c: relayout(c, *args) for c in capacities]
    panel, pairs = lax.switch(choice, branches, stored, snap_slot[None, :], other, chip, position)
    pairs = lax.optimization_barrier(pairs)
    pairs = lax.all_to_all(pairs, "store", split_axis=0, concat_axis=0, tiled=True)
    pairs = pl.pallas_call(sum_kernel, out_shape=float_array(rows, *pairs.shape[1:]), compiler_params=BIG)(pairs)
    pairs = lax.all_to_all(pairs, "rows", split_axis=0, concat_axis=0, tiled=True)
    modes, factor = pl.pallas_call(
        lambda *refs: modes_kernel(columns * store * rows, *refs),
        out_shape=(float_array(n, columns), float_array(n, n)),
        in_specs=[VMEM, ANY],
        out_specs=(ANY, VMEM),
        scratch_shapes=[pltpu.VMEM((n, columns), jnp.float32)] * 2 + [pltpu.SemaphoreType.DMA((9,))],
        compiler_params=BIG,
    )(pairs, panel)
    return (modes, factor)


def solution(mesh):
    in_specs = (P("store", "rows"), P())
    out_specs = (P(None, ("rows", "store")), P())
    return jax.shard_map(
        per_device, mesh=mesh, in_specs=in_specs, out_specs=out_specs, check_vma=False
    )
```

```python
import functools
import math

import jax
import jax.numpy as jnp
from jax import lax
from jax.experimental import pallas as pl
from jax.experimental.pallas import tpu as pltpu
from jax.sharding import PartitionSpec as P

HIGHEST = lax.Precision.HIGHEST
UP = 2.0**24


def dot(a, b):
    return jnp.dot(a, b, precision=HIGHEST, preferred_element_type=jnp.float32)


def iota(shape, dim):
    return lax.broadcasted_iota(jnp.int32, shape, dim)


def power_above(value):
    c, inverse = jnp.ones_like(value), jnp.ones_like(value)
    for e in (64, 32, 16, 8, 4, 2, 1):
        big = value * inverse > 2.0**e * 0.5
        c = jnp.where(big, c * 2.0**e, c)
        inverse = jnp.where(big, inverse * 2.0**-e, inverse)
    for e in (64, 32, 16, 8, 4, 2, 1):
        small = (value * inverse <= 2.0**-e) & (c > 2.0 ** (e - 126))
        c = jnp.where(small, c * 2.0**-e, c)
        inverse = jnp.where(small, inverse * 2.0**e, inverse)
    return c, inverse


def row_of(column):
    n = column.shape[0]
    return jnp.sum(jnp.where(iota((n, n), 0) == iota((n, n), 1), column, 0.0), axis=0, keepdims=True)


def two_sum(a, b):
    s = a + b
    t = s - a
    return s, (a - (s - t)) + (b - t)


def pair_add(first, second):
    s, e = two_sum(first[0], second[0])
    return s, (first[1] + second[1]) + e * UP


def nearest(x):
    return lax.round(x, lax.RoundingMethod.TO_NEAREST_EVEN)


def pieces(x, count):
    out = []
    t = x * 256.0
    for i in range(count):
        n = nearest(t)
        out.append(n)
        t = (t - n) * 512.0
    return out, t


def levels_to_pair(levels):
    hi, lo = levels[0], jnp.zeros_like(levels[0])
    for l in range(1, len(levels)):
        hi, e = two_sum(hi, levels[l] * 2.0 ** (-9 * l))
        lo = lo + e
    return two_sum(hi, lo)


def eliminate(gram, block=8):
    n = gram.shape[0]
    rows, columns = iota((n, n), 0), iota((n, n), 1)
    whole = jnp.concatenate([gram, (rows == columns).astype(jnp.float32)], axis=1)
    lane = iota((8, 2 * n), 1)
    sub = iota((8, 2 * n), 0)
    g = n // 8
    blocks = [whole[8 * i : 8 * i + 8] for i in range(g)]
    done = []
    for b in range(g):
        cols = {}
        for i in range(b, g):
            for q in range(8):
                j = 8 * b + q
                cols[i, q] = jnp.broadcast_to(blocks[i][:, j : j + 1], (8, 2 * n))
        mult = {}
        pivots = jnp.ones((8, 2 * n), jnp.float32)
        rowsb = blocks[b]

        def spread(value, q):
            return jnp.broadcast_to(value[q : q + 1], (8, 2 * n))

        for q in range(0, 8, 2):
            p, o, r = spread(cols[b, q], q), spread(cols[b, q + 1], q), spread(cols[b, q + 1], q + 1)
            determinant = p * r - o * o
            w, v = 1.0 / p, p * (1.0 / determinant)
            ratio = o * w
            for i in range(b, g):
                first = cols[i, q] * w
                second = (cols[i, q + 1] - cols[i, q] * ratio) * v
                if i == b:
                    first = jnp.where(sub > q, first, 0.0)
                    second = jnp.where(sub > q + 1, second, 0.0)
                mult[i, q], mult[i, q + 1] = first, second
            pivots = jnp.where(sub == q, p, jnp.where(sub == q + 1, r - o * ratio, pivots))
            row = spread(rowsb, q)
            rowsb = rowsb - mult[b, q] * row
            rowsb = rowsb - mult[b, q + 1] * spread(rowsb, q + 1)
            for c in range(q + 2, 8):
                a0 = spread(cols[b, c], q)
                a1 = spread(cols[b, c], q + 1) - ratio * a0
                for i in range(b, g):
                    cols[i, c] = (cols[i, c] - mult[i, q] * a0) - mult[i, q + 1] * a1
        for i in range(b + 1, g):
            value = blocks[i]
            for q in range(8):
                value = value - mult[i, q] * jnp.broadcast_to(rowsb[q : q + 1], (8, 2 * n))
            blocks[i] = value
        s = lax.rsqrt(pivots)
        s = s * (1.5 - 0.5 * pivots * s * s)
        done.append(rowsb * s)
    whole = jnp.concatenate(done, axis=0)
    upper = jnp.where(rows <= columns, whole[:, :n], 0.0)
    lower = jnp.where(rows >= columns, whole[:, n:], 0.0)
    return upper, lower


def bf16_dot(a, b):
    return lax.dot_general(a, b, (((1,), (0,)), ((), ())), preferred_element_type=jnp.float32)


def wide_product(left, right, keep):
    n = left[0].shape[0]
    na, nb = len(left), len(right)
    l = jnp.concatenate([x.astype(jnp.bfloat16) for x in left], axis=0)
    r = jnp.concatenate([x.astype(jnp.bfloat16) for x in right], axis=1)
    m = bf16_dot(l, r)
    out = []
    for lev in range(keep):
        acc = None
        for a in range(na):
            c = lev - a
            if 0 <= c < nb:
                t = m[a * n : (a + 1) * n, c * n : (c + 1) * n]
                acc = t if acc is None else acc + t
        out.append(acc)
    return out


def second_gram(hi, lo, lower):
    first, rest = pieces(hi, 3)
    rest = rest + lo * (2.0 ** (8 + 27) / UP)
    out = []
    for _ in range(3):
        n = nearest(rest)
        out.append(n)
        rest = (rest - n) * 512.0
    g = first + out
    top = jnp.max(jnp.abs(lower), axis=1, keepdims=True)
    u, v = power_above(top)
    ls, _ = pieces(lower * v, 4)
    lt = [x.T for x in ls]
    ur = row_of(u)
    lev = wide_product(g, lt, 7)
    ch, cl = levels_to_pair(lev)
    scale = ur * 2.0**-16
    ch, cl = ch * scale, cl * scale
    cs, rest = pieces(ch * 0.5, 3)
    rest = rest + cl * (0.5 * 2.0 ** (8 + 27))
    for _ in range(2):
        n = nearest(rest)
        cs.append(n)
        rest = (rest - n) * 512.0
    lev = wide_product(ls, cs, 7)
    h, l = levels_to_pair(lev)
    return (h + l) * (u * 2.0**-15)


def finish(hi, lo, count):
    n = hi.shape[0]
    eye = iota((n, n), 0) == iota((n, n), 1)
    diag = jnp.sum(jnp.where(eye, hi, 0.0), axis=1, keepdims=True)
    d, di = power_above(jnp.sqrt(diag))
    dr, dir_ = row_of(d), row_of(di)
    hs = (hi * di) * dir_
    ls = (lo * di) * dir_
    r1, l1 = eliminate(hs)
    g2 = second_gram(hs, ls, l1)
    r2, l2 = eliminate(g2)
    scale = math.sqrt(count)
    w = dot(l2, l1) * (dir_ * scale)
    factor = dot(r2, r1) * (dr * (1.0 / scale))
    return w, factor, g2


def combine(acc, c):
    n = acc.shape[0] // 3
    cr = row_of(c)
    part = [[acc[a * n : (a + 1) * n, b * n : (b + 1) * n] for b in range(4)] for a in range(3)]
    levels = []
    for lev in range(6):
        total = None
        for a in range(3):
            b = lev - a
            if 0 <= b < 4:
                x = part[a][b] + part[a][b].T if b == 3 else part[a][b]
                total = x if total is None else total + x
        levels.append(total)
    hi = jnp.zeros((n, n), jnp.float32)
    lo = jnp.zeros((n, n), jnp.float32)
    for lev, t in enumerate(levels):
        high = lax.shift_right_arithmetic(t, 14)
        low = (t - lax.shift_left(high, 14)).astype(jnp.float32) * 2.0 ** (-9 * lev)
        high = high.astype(jnp.float32) * 2.0 ** (14 - 9 * lev)
        hi, e = two_sum(hi, high)
        lo = lo + e
        hi, e = two_sum(hi, low)
        lo = lo + e
    hi, lo = two_sum(hi, lo)
    f = 2.0**-16
    return ((hi * f) * c) * cr, (((lo * (f * UP)) * c) * cr)


STEP = 256
CORES = 2
QUARTERS = 4
HALVES = 2
BIG = pltpu.CompilerParams(vmem_limit_bytes=8 * 2**20)
ANY = pl.BlockSpec(memory_space=pl.ANY)
HBM = pl.BlockSpec(memory_space=pltpu.HBM)
VMEM = pl.BlockSpec(memory_space=pltpu.VMEM)


def each(count, rolled, body, carry):
    if rolled:
        return lax.fori_loop(0, count, body, carry)
    for i in range(count):
        carry = body(i, carry)
    return carry


def columns_at(start):
    return pl.ds(start if isinstance(start, int) else pl.multiple_of(start, STEP), STEP)


def thirds(x):
    high = x.astype(jnp.bfloat16)
    rest = x - high.astype(jnp.float32)
    mid = rest.astype(jnp.bfloat16)
    low = (rest - mid.astype(jnp.float32)).astype(jnp.bfloat16)
    return jnp.concatenate([high, mid, low], axis=0)


def place():
    store = lax.axis_index("store")
    return store // CORES, store % CORES


def row_sum(mask_value):
    return jnp.sum(mask_value, axis=0, keepdims=True)


def positions(slot, span):
    n = slot.shape[1]
    column = jnp.sum(jnp.where(iota((n, n), 0) == iota((n, n), 1), slot, 0), axis=1, keepdims=True)
    before = (column < slot) & (column // span == slot // span)
    return slot // span, row_sum(before.astype(jnp.int32))


def part_kernel(distance, chips, stored_ref, out_ref, sem):
    columns = out_ref.shape[1]
    z, core = place()
    owner = lax.rem(z + distance, chips) * CORES + 1 - core
    start = pl.multiple_of(owner * columns, columns)
    copy = pltpu.make_async_copy(stored_ref.at[:, pl.ds(start, columns)], out_ref, sem)
    copy.start()
    copy.wait()


def pick_kernel(distance, passed, index, halves, chips, capacity, *refs):
    stored_ref, slot_ref, other_ref = refs[:3]
    sems = refs[-1]
    slots, columns = other_ref.shape[-2:]
    z, core = place()

    def part(d, c):
        owner = lax.rem(z + d, chips) * CORES + c
        return stored_ref.at[:, pl.ds(pl.multiple_of(owner * columns, columns), columns)]

    copies = []
    if passed:
        out_ref, parts_ref, own_ref, got_ref, held_ref, made_ref = refs[-7:-1]
        copies.append(pltpu.make_async_copy(part(distance, core), own_ref, sems.at[0]))
        copies.append(pltpu.make_async_copy(other_ref, got_ref, sems.at[1]))
        for i, d in enumerate(passed):
            copies.append(pltpu.make_async_copy(part(d, 1 - core), held_ref.at[i], sems.at[2 + i]))
    else:
        outs, (own_ref, got_ref) = refs[-3 - halves : -3], refs[-3:-1]
        copies.append(pltpu.make_async_copy(part(distance, core), own_ref, sems.at[0]))
        copies.append(pltpu.make_async_copy(other_ref.at[index], got_ref, sems.at[1]))
    for copy in copies:
        copy.start()
    slot = slot_ref[...]
    span = CORES * slots
    chip, position = positions(slot, span)
    local = slot - (chip * CORES + core) * slots
    local = jnp.where(local < 0, local + span, local)
    count = slot.shape[1]
    rows = QUARTERS * capacity
    row, column = iota((rows, count), 0), iota((span, count), 0)
    quarter = sum((row >= q * capacity).astype(jnp.int32) for q in range(1, QUARTERS))
    ranks = ((chip == z) & (position == row - quarter * capacity)).astype(jnp.bfloat16)
    locals_ = (local == column).astype(jnp.bfloat16)
    locals_ = jnp.concatenate([locals_] * QUARTERS, axis=0)
    hit = lax.dot_general(ranks, locals_, (((1,), (1,)), ((), ())), preferred_element_type=jnp.float32)
    shape = (rows, QUARTERS * span)
    quarter = sum((iota(shape, 0) >= q * capacity).astype(jnp.int32) for q in range(1, QUARTERS))
    selector = jnp.where(quarter == iota(shape, 1) // span, hit, 0.0).astype(jnp.bfloat16)
    selector = jnp.concatenate([selector] * 3, axis=1)
    wide = columns // QUARTERS

    def step(out, first, i, carry):
        at = [columns_at(q * wide + first + i * STEP) for q in range(QUARTERS)]
        both = [ref[:, part] for part in at for ref in (own_ref, got_ref)]
        out[:, columns_at(i * STEP)] = bf16_dot(selector, thirds(jnp.concatenate(both, axis=0)))
        return carry

    if not passed:
        for copy in copies:
            copy.wait()
        for h, out in enumerate(outs):
            each(out.shape[1] // STEP, True, functools.partial(step, out, h * out.shape[1]), 0)
        return
    copies[0].wait()
    copies[1].wait()
    half = wide // 2
    ends = []
    for h in range(2):
        part = pl.ds(h * half, half)
        each(half // STEP, capacity == CORES * slots, functools.partial(step, made_ref.at[:, part], h * half), 0)
        ends.append(pltpu.make_async_copy(made_ref.at[:, part], out_ref.at[:, part], sems.at[h]))
        ends[-1].start()
        if h == 0:
            for i in range(len(passed)):
                copies[2 + i].wait()
                ends.append(pltpu.make_async_copy(held_ref.at[i], parts_ref.at[i], sems.at[2 + i]))
                ends[-1].start()
    for end in ends:
        end.wait()


def picked(distance, halves, chips, capacity, stored, slot, others, index, *after):
    _, slots, columns = others.shape
    return pl.pallas_call(
        lambda *refs: pick_kernel(distance, (), index, halves, chips, capacity, *refs),
        out_shape=(float_array(QUARTERS * capacity, columns // QUARTERS // halves),) * halves,
        in_specs=[HBM, VMEM, ANY] + [ANY] * len(after),
        scratch_shapes=[pltpu.VMEM((slots, columns), jnp.float32)] * 2 + [pltpu.SemaphoreType.DMA((2,))],
        compiler_params=BIG,
    )(stored, slot, others, *after)


def picked_first(distance, passed, chips, capacity, stored, slot, other):
    slots, columns = other.shape
    count = len(passed)
    return pl.pallas_call(
        lambda *refs: pick_kernel(distance, passed, None, 1, chips, capacity, *refs),
        out_shape=(float_array(QUARTERS * capacity, columns // QUARTERS), float_array(count, slots, columns)),
        in_specs=[HBM, VMEM, ANY],
        out_specs=(ANY, ANY),
        scratch_shapes=[
            pltpu.VMEM((slots, columns), jnp.float32),
            pltpu.VMEM((slots, columns), jnp.float32),
            pltpu.VMEM((count, slots, columns), jnp.float32),
            pltpu.VMEM((QUARTERS * capacity, columns // QUARTERS), jnp.float32),
            pltpu.SemaphoreType.DMA((2 + count,)),
        ],
        compiler_params=pltpu.CompilerParams(vmem_limit_bytes=5 * 2**20),
    )(stored, slot, other)


def swap(part):
    return lax.ppermute(part, "store", [(i, i ^ 1) for i in range(lax.axis_size("store"))])


def send(block, d):
    store = lax.axis_size("store")
    return lax.ppermute(block, "store", [(i, (i + d * CORES) % store) for i in range(store)])


def ordered(parts, selector):
    return bf16_dot(selector, thirds(jnp.concatenate(parts, axis=0)))


def order_kernel(blocks, *refs):
    block_refs, selector_ref, ready_refs, out_ref = refs[:blocks], refs[blocks], refs[blocks + 1 : -1], refs[-1]
    selector = selector_ref[...]

    def step(i, carry):
        part = columns_at(i * STEP)
        got = ordered([ref[:, part] for ref in block_refs], selector)
        for ref in ready_refs:
            got = got + ref[:, part]
        out_ref[:, part] = got
        return carry

    each(out_ref.shape[1] // STEP, True, step, 0)


def gram_kernel(rolled, *refs):
    first_ref, second_ref, selector_ref, done_ref, ready_ref, panel_ref, out_ref, held_ref, panel_held, sems = refs
    n, columns = panel_ref.shape
    wide = columns // QUARTERS

    fetches = []
    for j, ref in enumerate((first_ref, second_ref)):
        fetches.append(pltpu.make_async_copy(ref, held_ref.at[j], sems.at[0, j]))
        fetches[-1].start()
    selector = selector_ref[...]

    blocks = wide // STEP
    done = blocks // HALVES

    def place_rows(i, got, top):
        for q in range(QUARTERS):
            rows = got[q * n : (q + 1) * n]
            panel_held[:, columns_at(q * wide + i * STEP)] = rows
            top = jnp.maximum(top, jnp.abs(rows))
        return top

    def gather(i, top):
        part = columns_at(i * STEP)
        got = ordered([held_ref[0, :, part], held_ref[1, :, part]], selector)
        return place_rows(done + i, got + ready_ref[:, columns_at((done + i) * STEP)], top)

    top = jnp.zeros((n, STEP), jnp.float32)
    top = each(done, rolled, lambda i, top: place_rows(i, done_ref[:, columns_at(i * STEP)], top), top)
    for fetch in fetches:
        fetch.wait()
    top = each(blocks - done, rolled, gather, top)
    copies = []
    for q in range(QUARTERS):
        part = pl.ds(q * wide, wide)
        copies.append(pltpu.make_async_copy(panel_held.at[:, part], panel_ref.at[:, part], sems.at[1, q]))
        copies[-1].start()
    c, inverse = power_above(jnp.max(top, axis=1, keepdims=True))

    def step(i, carry):
        parts, _ = pieces(panel_held[:, columns_at(i * STEP)] * inverse, 4)
        x = jnp.concatenate([p.astype(jnp.bfloat16) for p in parts], axis=0)
        h = lax.dot_general(x[: 3 * n], x, (((1,), (1,)), ((), ())), preferred_element_type=jnp.float32)
        return carry + h.astype(jnp.int32)

    total = each(columns // STEP, rolled, step, jnp.zeros((3 * n, 4 * n), jnp.int32))
    packed = pack(*combine(total, c))
    for i in range(out_ref.shape[0]):
        out_ref[i] = packed
    for copy in copies:
        copy.wait()


def pack(hi, lo):
    h = hi.shape[0] // 2
    rows, columns = iota((h, h), 0), iota((h, h), 1)
    wide, diagonals = [], []
    for x in (hi, lo):
        a, b, c = x[:h, :h], x[:h, h:], x[h:, h:]
        diagonal = jnp.sum(jnp.where(rows == columns, c, 0.0), axis=0, keepdims=True)
        wide += [jnp.where(columns >= rows, a, c), b]
        diagonals += [diagonal, jnp.zeros_like(diagonal)]
    tail = jnp.broadcast_to(jnp.concatenate(diagonals, axis=1), (8, 4 * h))
    return jnp.concatenate([jnp.concatenate(wide, axis=1), tail], axis=0)


def unpack(packed):
    h = packed.shape[1] // 4
    rows, columns = iota((h, h), 0), iota((h, h), 1)
    main = packed[:h]
    turned = main.T
    out = []
    for i in (0, 2 * h):
        m, mt = main[:, i : i + h], turned[i : i + h]
        b, bt = main[:, i + h : i + 2 * h], turned[i + h : i + 2 * h]
        a = jnp.where(columns >= rows, m, mt)
        c = jnp.where(columns < rows, m, jnp.where(columns > rows, mt, packed[h : h + 1, i : i + h]))
        out.append(jnp.concatenate([jnp.concatenate([a, b], axis=1), jnp.concatenate([bt, c], axis=1)], axis=0))
    return out


def pair_sum(ref):
    half = ref.shape[2] // 2
    terms = [(ref[i], None) for i in range(ref.shape[0])]
    while len(terms) > 1:
        merged = []
        for (x, a), (y, b) in zip(terms[::2], terms[1::2]):
            total, e = two_sum(x, y)
            merged.append((total, e if a is None else (a + b) + e))
        terms = merged
    total, rest = terms[0]
    rest = jnp.where(iota(total.shape, 1) < half, rest * UP, 0.0)
    return total + pltpu.roll(rest, half, 1)


def sum_kernel(in_ref, out_ref):
    total = pair_sum(in_ref)
    for i in range(out_ref.shape[0]):
        out_ref[i] = total


def modes_kernel(count, pairs_ref, panel_ref, out_ref, factor_ref, panel_held, out_held, sems):
    fetch = pltpu.make_async_copy(panel_ref, panel_held, sems.at[sems.shape[0] - 1])
    fetch.start()
    weights, factor, _ = finish(*unpack(pair_sum(pairs_ref)), count)
    factor_ref[...] = factor
    n = weights.shape[0]
    w = thirds(weights)
    first, second, third = w[:n], w[n : 2 * n], w[2 * n :]
    none = jnp.zeros_like(first)
    left = jnp.concatenate(
        [
            jnp.concatenate([first, first, first], axis=1),
            jnp.concatenate([second, second, none], axis=1),
            jnp.concatenate([third, none, none], axis=1),
        ],
        axis=0,
    )
    fetch.wait()
    chunks = sems.shape[0] - 1
    wide = out_ref.shape[1] // chunks
    copies = []
    for i in range(chunks):
        for k in range(i * wide, (i + 1) * wide, STEP):
            got = bf16_dot(left, thirds(panel_held[:, k : k + STEP]))
            out_held[:, k : k + STEP] = (got[2 * n :] + got[n : 2 * n]) + got[:n]
        part = pl.ds(i * wide, wide)
        copies.append(pltpu.make_async_copy(out_held.at[:, part], out_ref.at[:, part], sems.at[i]))
        copies[-1].start()
    for copy in copies:
        copy.wait()


def float_array(*shape):
    return jax.ShapeDtypeStruct(shape, jnp.float32)


def relayout(capacity, stored, slot, other, chip, position):
    n = chip.shape[0]
    store = lax.axis_size("store")
    chips, columns = store // CORES, other.shape[1]
    z, _ = place()
    far, near = chips // 2, (1, chips - 1)
    rest = (*near, 0)
    block, parts = picked_first(far, rest, chips, capacity, stored, slot, other)
    blocks = {far: send(block, far)}
    others = swap(parts)
    for i, d in enumerate(rest):
        made = picked(d, HALVES if d else 1, chips, capacity, stored, slot, others, i, block)
        block = made[0]
        blocks[d] = [send(half, d) for half in made] if d else block
    distance = lax.rem(z - chip + chips, chips)
    first, last = (0, far), near

    def selector(distances):
        source = sum(jnp.where(distance == d, i + 1, 0) for i, d in enumerate(distances)) - 1
        source = jnp.where(source < 0, -(QUARTERS * capacity), source * QUARTERS * capacity + position)
        source = source[None, :] + jnp.arange(QUARTERS)[:, None] * capacity
        hit = source.reshape(-1)[:, None] == jnp.arange(len(distances) * QUARTERS * capacity)[None, :]
        return jnp.tile(hit.astype(jnp.bfloat16), (1, 3))

    def in_order(size, parts, selector, *ready):
        return pl.pallas_call(
            lambda *refs: order_kernel(len(parts), *refs),
            out_shape=float_array(QUARTERS * n, size),
            compiler_params=BIG,
        )(*parts, selector, *ready)

    wide = columns // QUARTERS
    ready = in_order(wide, [blocks[d] for d in first], selector(first))
    last = selector(last)
    done = in_order(wide // HALVES, [blocks[d][0] for d in near], last, ready)
    shape = blocks[near[0]][1].shape
    return pl.pallas_call(
        lambda *refs: gram_kernel(capacity == CORES * stored.shape[0], *refs),
        out_shape=(float_array(n, columns), float_array(store, n // 2 + 8, 2 * n)),
        in_specs=[ANY, ANY, VMEM, VMEM, VMEM],
        out_specs=(ANY, VMEM),
        scratch_shapes=[
            pltpu.VMEM((2, *shape), jnp.float32),
            pltpu.VMEM((n, columns), jnp.float32),
            pltpu.SemaphoreType.DMA((2, QUARTERS)),
        ],
        compiler_params=BIG,
    )(*[blocks[d][1] for d in near], last, done, ready)


def per_device(stored, snap_slot):
    n = snap_slot.shape[0]
    slots = stored.shape[0]
    store, rows = lax.axis_size("store"), lax.axis_size("rows")
    columns, chips = stored.shape[1] // store, store // CORES
    part = pl.pallas_call(
        lambda *refs: part_kernel(chips // 2, chips, *refs),
        out_shape=float_array(slots, columns),
        in_specs=[HBM],
        scratch_shapes=[pltpu.SemaphoreType.DMA(())],
        compiler_params=BIG,
    )(stored)
    other = swap(part)
    chip = snap_slot // (slots * CORES)
    same = chip[:, None] == chip[None, :]
    position = jnp.sum((same & (snap_slot[None, :] < snap_slot[:, None])).astype(jnp.int32), axis=1)
    most = jnp.max(position) + 1
    capacities = (22, 24, 26, 32)
    choice = sum((most > c).astype(jnp.int32) for c in capacities[:-1])
    branches = [lambda *args, c=c: relayout(c, *args) for c in capacities]
    panel, pairs = lax.switch(choice, branches, stored, snap_slot[None, :], other, chip, position)
    pairs = lax.optimization_barrier(pairs)
    pairs = lax.all_to_all(pairs, "store", split_axis=0, concat_axis=0, tiled=True)
    pairs = pl.pallas_call(sum_kernel, out_shape=float_array(rows, *pairs.shape[1:]), compiler_params=BIG)(pairs)
    pairs = lax.all_to_all(pairs, "rows", split_axis=0, concat_axis=0, tiled=True)
    modes, factor = pl.pallas_call(
        lambda *refs: modes_kernel(columns * store * rows, *refs),
        out_shape=(float_array(n, columns), float_array(n, n)),
        in_specs=[VMEM, ANY],
        out_specs=(ANY, VMEM),
        scratch_shapes=[pltpu.VMEM((n, columns), jnp.float32)] * 2 + [pltpu.SemaphoreType.DMA((9,))],
        compiler_params=BIG,
    )(pairs, panel)
    return (modes, factor)


def solution(mesh):
    in_specs = (P("store", "rows"), P())
    out_specs = (P(None, ("rows", "store")), P())
    return jax.shard_map(
        per_device, mesh=mesh, in_specs=in_specs, out_specs=out_specs, check_vma=False
    )
```

```python
import functools
import math

import jax
import jax.numpy as jnp
from jax import lax
from jax.experimental import pallas as pl
from jax.experimental.pallas import tpu as pltpu
from jax.sharding import PartitionSpec as P

HIGHEST = lax.Precision.HIGHEST
UP = 2.0**24


def dot(a, b):
    return jnp.dot(a, b, precision=HIGHEST, preferred_element_type=jnp.float32)


def iota(shape, dim):
    return lax.broadcasted_iota(jnp.int32, shape, dim)


def power_above(value):
    c, inverse = jnp.ones_like(value), jnp.ones_like(value)
    for e in (64, 32, 16, 8, 4, 2, 1):
        big = value * inverse > 2.0**e * 0.5
        c = jnp.where(big, c * 2.0**e, c)
        inverse = jnp.where(big, inverse * 2.0**-e, inverse)
    for e in (64, 32, 16, 8, 4, 2, 1):
        small = (value * inverse <= 2.0**-e) & (c > 2.0 ** (e - 126))
        c = jnp.where(small, c * 2.0**-e, c)
        inverse = jnp.where(small, inverse * 2.0**e, inverse)
    return c, inverse


def row_of(column):
    n = column.shape[0]
    return jnp.sum(jnp.where(iota((n, n), 0) == iota((n, n), 1), column, 0.0), axis=0, keepdims=True)


def two_sum(a, b):
    s = a + b
    t = s - a
    return s, (a - (s - t)) + (b - t)


def pair_add(first, second):
    s, e = two_sum(first[0], second[0])
    return s, (first[1] + second[1]) + e * UP


def nearest(x):
    return lax.round(x, lax.RoundingMethod.TO_NEAREST_EVEN)


def pieces(x, count):
    out = []
    t = x * 256.0
    for i in range(count):
        n = nearest(t)
        out.append(n)
        t = (t - n) * 512.0
    return out, t


def levels_to_pair(levels):
    hi, lo = levels[0], jnp.zeros_like(levels[0])
    for l in range(1, len(levels)):
        hi, e = two_sum(hi, levels[l] * 2.0 ** (-9 * l))
        lo = lo + e
    return two_sum(hi, lo)


def eliminate(gram, block=8):
    n = gram.shape[0]
    rows, columns = iota((n, n), 0), iota((n, n), 1)
    whole = jnp.concatenate([gram, (rows == columns).astype(jnp.float32)], axis=1)
    lane = iota((8, 2 * n), 1)
    sub = iota((8, 2 * n), 0)
    g = n // 8
    blocks = [whole[8 * i : 8 * i + 8] for i in range(g)]
    done = []
    for b in range(g):
        cols = {}
        for i in range(b, g):
            for q in range(8):
                j = 8 * b + q
                cols[i, q] = jnp.broadcast_to(blocks[i][:, j : j + 1], (8, 2 * n))
        mult = {}
        pivots = jnp.ones((8, 2 * n), jnp.float32)
        rowsb = blocks[b]

        def spread(value, q):
            return jnp.broadcast_to(value[q : q + 1], (8, 2 * n))

        for q in range(0, 8, 2):
            p, o, r = spread(cols[b, q], q), spread(cols[b, q + 1], q), spread(cols[b, q + 1], q + 1)
            determinant = p * r - o * o
            w, v = 1.0 / p, p * (1.0 / determinant)
            ratio = o * w
            for i in range(b, g):
                first = cols[i, q] * w
                second = (cols[i, q + 1] - cols[i, q] * ratio) * v
                if i == b:
                    first = jnp.where(sub > q, first, 0.0)
                    second = jnp.where(sub > q + 1, second, 0.0)
                mult[i, q], mult[i, q + 1] = first, second
            pivots = jnp.where(sub == q, p, jnp.where(sub == q + 1, r - o * ratio, pivots))
            row = spread(rowsb, q)
            rowsb = rowsb - mult[b, q] * row
            rowsb = rowsb - mult[b, q + 1] * spread(rowsb, q + 1)
            for c in range(q + 2, 8):
                a0 = spread(cols[b, c], q)
                a1 = spread(cols[b, c], q + 1) - ratio * a0
                for i in range(b, g):
                    cols[i, c] = (cols[i, c] - mult[i, q] * a0) - mult[i, q + 1] * a1
        for i in range(b + 1, g):
            value = blocks[i]
            for q in range(8):
                value = value - mult[i, q] * jnp.broadcast_to(rowsb[q : q + 1], (8, 2 * n))
            blocks[i] = value
        s = lax.rsqrt(pivots)
        s = s * (1.5 - 0.5 * pivots * s * s)
        done.append(rowsb * s)
    whole = jnp.concatenate(done, axis=0)
    upper = jnp.where(rows <= columns, whole[:, :n], 0.0)
    lower = jnp.where(rows >= columns, whole[:, n:], 0.0)
    return upper, lower


def bf16_dot(a, b):
    return lax.dot_general(a, b, (((1,), (0,)), ((), ())), preferred_element_type=jnp.float32)


def wide_product(left, right, keep):
    n = left[0].shape[0]
    na, nb = len(left), len(right)
    l = jnp.concatenate([x.astype(jnp.bfloat16) for x in left], axis=0)
    r = jnp.concatenate([x.astype(jnp.bfloat16) for x in right], axis=1)
    m = bf16_dot(l, r)
    out = []
    for lev in range(keep):
        acc = None
        for a in range(na):
            c = lev - a
            if 0 <= c < nb:
                t = m[a * n : (a + 1) * n, c * n : (c + 1) * n]
                acc = t if acc is None else acc + t
        out.append(acc)
    return out


def second_gram(hi, lo, lower):
    first, rest = pieces(hi, 3)
    rest = rest + lo * (2.0 ** (8 + 27) / UP)
    out = []
    for _ in range(3):
        n = nearest(rest)
        out.append(n)
        rest = (rest - n) * 512.0
    g = first + out
    top = jnp.max(jnp.abs(lower), axis=1, keepdims=True)
    u, v = power_above(top)
    ls, _ = pieces(lower * v, 4)
    lt = [x.T for x in ls]
    ur = row_of(u)
    lev = wide_product(g, lt, 7)
    ch, cl = levels_to_pair(lev)
    scale = ur * 2.0**-16
    ch, cl = ch * scale, cl * scale
    cs, rest = pieces(ch * 0.5, 3)
    rest = rest + cl * (0.5 * 2.0 ** (8 + 27))
    for _ in range(2):
        n = nearest(rest)
        cs.append(n)
        rest = (rest - n) * 512.0
    lev = wide_product(ls, cs, 7)
    h, l = levels_to_pair(lev)
    return (h + l) * (u * 2.0**-15)


def finish(hi, lo, count):
    n = hi.shape[0]
    eye = iota((n, n), 0) == iota((n, n), 1)
    diag = jnp.sum(jnp.where(eye, hi, 0.0), axis=1, keepdims=True)
    d, di = power_above(jnp.sqrt(diag))
    dr, dir_ = row_of(d), row_of(di)
    hs = (hi * di) * dir_
    ls = (lo * di) * dir_
    r1, l1 = eliminate(hs)
    g2 = second_gram(hs, ls, l1)
    r2, l2 = eliminate(g2)
    scale = math.sqrt(count)
    w = dot(l2, l1) * (dir_ * scale)
    factor = dot(r2, r1) * (dr * (1.0 / scale))
    return w, factor, g2


def combine(acc, c):
    n = acc.shape[0] // 3
    cr = row_of(c)
    part = [[acc[a * n : (a + 1) * n, b * n : (b + 1) * n] for b in range(4)] for a in range(3)]
    levels = []
    for lev in range(6):
        total = None
        for a in range(3):
            b = lev - a
            if 0 <= b < 4:
                x = part[a][b] + part[a][b].T if b == 3 else part[a][b]
                total = x if total is None else total + x
        levels.append(total)
    hi = jnp.zeros((n, n), jnp.float32)
    lo = jnp.zeros((n, n), jnp.float32)
    for lev, t in enumerate(levels):
        high = lax.shift_right_arithmetic(t, 14)
        low = (t - lax.shift_left(high, 14)).astype(jnp.float32) * 2.0 ** (-9 * lev)
        high = high.astype(jnp.float32) * 2.0 ** (14 - 9 * lev)
        hi, e = two_sum(hi, high)
        lo = lo + e
        hi, e = two_sum(hi, low)
        lo = lo + e
    hi, lo = two_sum(hi, lo)
    f = 2.0**-16
    return ((hi * f) * c) * cr, (((lo * (f * UP)) * c) * cr)


STEP = 256
CORES = 2
QUARTERS = 4
HALVES = 2
BIG = pltpu.CompilerParams(vmem_limit_bytes=8 * 2**20)
ANY = pl.BlockSpec(memory_space=pl.ANY)
HBM = pl.BlockSpec(memory_space=pltpu.HBM)
VMEM = pl.BlockSpec(memory_space=pltpu.VMEM)


def each(count, rolled, body, carry):
    if rolled:
        return lax.fori_loop(0, count, body, carry)
    for i in range(count):
        carry = body(i, carry)
    return carry


def columns_at(start):
    return pl.ds(start if isinstance(start, int) else pl.multiple_of(start, STEP), STEP)


def thirds(x):
    high = x.astype(jnp.bfloat16)
    rest = x - high.astype(jnp.float32)
    mid = rest.astype(jnp.bfloat16)
    low = (rest - mid.astype(jnp.float32)).astype(jnp.bfloat16)
    return jnp.concatenate([high, mid, low], axis=0)


def place():
    store = lax.axis_index("store")
    return store // CORES, store % CORES


def row_sum(mask_value):
    return jnp.sum(mask_value, axis=0, keepdims=True)


def positions(slot, span):
    n = slot.shape[1]
    column = jnp.sum(jnp.where(iota((n, n), 0) == iota((n, n), 1), slot, 0), axis=1, keepdims=True)
    before = (column < slot) & (column // span == slot // span)
    return slot // span, row_sum(before.astype(jnp.int32))


def part_kernel(distance, chips, stored_ref, out_ref, sem):
    columns = out_ref.shape[1]
    z, core = place()
    owner = lax.rem(z + distance, chips) * CORES + 1 - core
    start = pl.multiple_of(owner * columns, columns)
    copy = pltpu.make_async_copy(stored_ref.at[:, pl.ds(start, columns)], out_ref, sem)
    copy.start()
    copy.wait()


def pick_kernel(distance, passed, index, halves, chips, capacity, *refs):
    stored_ref, slot_ref, other_ref = refs[:3]
    sems = refs[-1]
    slots, columns = other_ref.shape[-2:]
    z, core = place()

    def part(d, c):
        owner = lax.rem(z + d, chips) * CORES + c
        return stored_ref.at[:, pl.ds(pl.multiple_of(owner * columns, columns), columns)]

    copies = []
    if passed:
        out_ref, parts_ref, own_ref, got_ref, held_ref, made_ref = refs[-7:-1]
        copies.append(pltpu.make_async_copy(part(distance, core), own_ref, sems.at[0]))
        copies.append(pltpu.make_async_copy(other_ref, got_ref, sems.at[1]))
        for i, d in enumerate(passed):
            copies.append(pltpu.make_async_copy(part(d, 1 - core), held_ref.at[i], sems.at[2 + i]))
    else:
        outs, (own_ref, got_ref) = refs[-3 - halves : -3], refs[-3:-1]
        copies.append(pltpu.make_async_copy(part(distance, core), own_ref, sems.at[0]))
        copies.append(pltpu.make_async_copy(other_ref.at[index], got_ref, sems.at[1]))
    for copy in copies:
        copy.start()
    slot = slot_ref[...]
    span = CORES * slots
    chip, position = positions(slot, span)
    local = slot - (chip * CORES + core) * slots
    local = jnp.where(local < 0, local + span, local)
    count = slot.shape[1]
    rows = QUARTERS * capacity
    row, column = iota((rows, count), 0), iota((span, count), 0)
    quarter = sum((row >= q * capacity).astype(jnp.int32) for q in range(1, QUARTERS))
    ranks = ((chip == z) & (position == row - quarter * capacity)).astype(jnp.bfloat16)
    locals_ = (local == column).astype(jnp.bfloat16)
    locals_ = jnp.concatenate([locals_] * QUARTERS, axis=0)
    hit = lax.dot_general(ranks, locals_, (((1,), (1,)), ((), ())), preferred_element_type=jnp.float32)
    shape = (rows, QUARTERS * span)
    quarter = sum((iota(shape, 0) >= q * capacity).astype(jnp.int32) for q in range(1, QUARTERS))
    selector = jnp.where(quarter == iota(shape, 1) // span, hit, 0.0).astype(jnp.bfloat16)
    selector = jnp.concatenate([selector] * 3, axis=1)
    wide = columns // QUARTERS

    def step(out, first, i, carry):
        at = [columns_at(q * wide + first + i * STEP) for q in range(QUARTERS)]
        both = [ref[:, part] for part in at for ref in (own_ref, got_ref)]
        out[:, columns_at(i * STEP)] = bf16_dot(selector, thirds(jnp.concatenate(both, axis=0)))
        return carry

    if not passed:
        for copy in copies:
            copy.wait()
        for h, out in enumerate(outs):
            each(out.shape[1] // STEP, True, functools.partial(step, out, h * out.shape[1]), 0)
        return
    copies[0].wait()
    copies[1].wait()
    half = wide // 2
    ends = []
    for h in range(2):
        part = pl.ds(h * half, half)
        each(half // STEP, capacity == CORES * slots, functools.partial(step, made_ref.at[:, part], h * half), 0)
        ends.append(pltpu.make_async_copy(made_ref.at[:, part], out_ref.at[:, part], sems.at[h]))
        ends[-1].start()
        if h == 0:
            for i in range(len(passed)):
                copies[2 + i].wait()
                ends.append(pltpu.make_async_copy(held_ref.at[i], parts_ref.at[i], sems.at[2 + i]))
                ends[-1].start()
    for end in ends:
        end.wait()


def picked(distance, halves, chips, capacity, stored, slot, others, index, *after):
    _, slots, columns = others.shape
    return pl.pallas_call(
        lambda *refs: pick_kernel(distance, (), index, halves, chips, capacity, *refs),
        out_shape=(float_array(QUARTERS * capacity, columns // QUARTERS // halves),) * halves,
        in_specs=[HBM, VMEM, ANY] + [ANY] * len(after),
        scratch_shapes=[pltpu.VMEM((slots, columns), jnp.float32)] * 2 + [pltpu.SemaphoreType.DMA((2,))],
        compiler_params=BIG,
    )(stored, slot, others, *after)


def picked_first(distance, passed, chips, capacity, stored, slot, other):
    slots, columns = other.shape
    count = len(passed)
    return pl.pallas_call(
        lambda *refs: pick_kernel(distance, passed, None, 1, chips, capacity, *refs),
        out_shape=(float_array(QUARTERS * capacity, columns // QUARTERS), float_array(count, slots, columns)),
        in_specs=[HBM, VMEM, ANY],
        out_specs=(ANY, ANY),
        scratch_shapes=[
            pltpu.VMEM((slots, columns), jnp.float32),
            pltpu.VMEM((slots, columns), jnp.float32),
            pltpu.VMEM((count, slots, columns), jnp.float32),
            pltpu.VMEM((QUARTERS * capacity, columns // QUARTERS), jnp.float32),
            pltpu.SemaphoreType.DMA((2 + count,)),
        ],
        compiler_params=pltpu.CompilerParams(vmem_limit_bytes=56 * 2**20),
    )(stored, slot, other)


def swap(part):
    return lax.ppermute(part, "store", [(i, i ^ 1) for i in range(lax.axis_size("store"))])


def send(block, d):
    store = lax.axis_size("store")
    return lax.ppermute(block, "store", [(i, (i + d * CORES) % store) for i in range(store)])


def ordered(parts, selector):
    return bf16_dot(selector, thirds(jnp.concatenate(parts, axis=0)))


def order_kernel(blocks, *refs):
    block_refs, selector_ref, ready_refs, out_ref = refs[:blocks], refs[blocks], refs[blocks + 1 : -1], refs[-1]
    selector = selector_ref[...]

    def step(i, carry):
        part = columns_at(i * STEP)
        got = ordered([ref[:, part] for ref in block_refs], selector)
        for ref in ready_refs:
            got = got + ref[:, part]
        out_ref[:, part] = got
        return carry

    each(out_ref.shape[1] // STEP, True, step, 0)


def gram_kernel(rolled, *refs):
    first_ref, second_ref, selector_ref, done_ref, ready_ref, panel_ref, out_ref, held_ref, panel_held, sems = refs
    n, columns = panel_ref.shape
    wide = columns // QUARTERS

    fetches = []
    for j, ref in enumerate((first_ref, second_ref)):
        fetches.append(pltpu.make_async_copy(ref, held_ref.at[j], sems.at[0, j]))
        fetches[-1].start()
    selector = selector_ref[...]

    blocks = wide // STEP
    done = blocks // HALVES

    def place_rows(i, got, top):
        for q in range(QUARTERS):
            rows = got[q * n : (q + 1) * n]
            panel_held[:, columns_at(q * wide + i * STEP)] = rows
            top = jnp.maximum(top, jnp.abs(rows))
        return top

    def gather(i, top):
        part = columns_at(i * STEP)
        got = ordered([held_ref[0, :, part], held_ref[1, :, part]], selector)
        return place_rows(done + i, got + ready_ref[:, columns_at((done + i) * STEP)], top)

    top = jnp.zeros((n, STEP), jnp.float32)
    top = each(done, rolled, lambda i, top: place_rows(i, done_ref[:, columns_at(i * STEP)], top), top)
    for fetch in fetches:
        fetch.wait()
    top = each(blocks - done, rolled, gather, top)
    copies = []
    for q in range(QUARTERS):
        part = pl.ds(q * wide, wide)
        copies.append(pltpu.make_async_copy(panel_held.at[:, part], panel_ref.at[:, part], sems.at[1, q]))
        copies[-1].start()
    c, inverse = power_above(jnp.max(top, axis=1, keepdims=True))

    def step(i, carry):
        parts, _ = pieces(panel_held[:, columns_at(i * STEP)] * inverse, 4)
        x = jnp.concatenate([p.astype(jnp.bfloat16) for p in parts], axis=0)
        h = lax.dot_general(x[: 3 * n], x, (((1,), (1,)), ((), ())), preferred_element_type=jnp.float32)
        return carry + h.astype(jnp.int32)

    total = each(columns // STEP, rolled, step, jnp.zeros((3 * n, 4 * n), jnp.int32))
    packed = pack(*combine(total, c))
    for i in range(out_ref.shape[0]):
        out_ref[i] = packed
    for copy in copies:
        copy.wait()


def pack(hi, lo):
    h = hi.shape[0] // 2
    rows, columns = iota((h, h), 0), iota((h, h), 1)
    wide, diagonals = [], []
    for x in (hi, lo):
        a, b, c = x[:h, :h], x[:h, h:], x[h:, h:]
        diagonal = jnp.sum(jnp.where(rows == columns, c, 0.0), axis=0, keepdims=True)
        wide += [jnp.where(columns >= rows, a, c), b]
        diagonals += [diagonal, jnp.zeros_like(diagonal)]
    tail = jnp.broadcast_to(jnp.concatenate(diagonals, axis=1), (8, 4 * h))
    return jnp.concatenate([jnp.concatenate(wide, axis=1), tail], axis=0)


def unpack(packed):
    h = packed.shape[1] // 4
    rows, columns = iota((h, h), 0), iota((h, h), 1)
    main = packed[:h]
    turned = main.T
    out = []
    for i in (0, 2 * h):
        m, mt = main[:, i : i + h], turned[i : i + h]
        b, bt = main[:, i + h : i + 2 * h], turned[i + h : i + 2 * h]
        a = jnp.where(columns >= rows, m, mt)
        c = jnp.where(columns < rows, m, jnp.where(columns > rows, mt, packed[h : h + 1, i : i + h]))
        out.append(jnp.concatenate([jnp.concatenate([a, b], axis=1), jnp.concatenate([bt, c], axis=1)], axis=0))
    return out


def pair_sum(ref):
    half = ref.shape[2] // 2
    terms = [(ref[i], None) for i in range(ref.shape[0])]
    while len(terms) > 1:
        merged = []
        for (x, a), (y, b) in zip(terms[::2], terms[1::2]):
            total, e = two_sum(x, y)
            merged.append((total, e if a is None else (a + b) + e))
        terms = merged
    total, rest = terms[0]
    rest = jnp.where(iota(total.shape, 1) < half, rest * UP, 0.0)
    return total + pltpu.roll(rest, half, 1)


def sum_kernel(in_ref, out_ref):
    total = pair_sum(in_ref)
    for i in range(out_ref.shape[0]):
        out_ref[i] = total


def modes_kernel(count, pairs_ref, panel_ref, out_ref, factor_ref, panel_held, out_held, sems):
    fetch = pltpu.make_async_copy(panel_ref, panel_held, sems.at[sems.shape[0] - 1])
    fetch.start()
    weights, factor, _ = finish(*unpack(pair_sum(pairs_ref)), count)
    factor_ref[...] = factor
    n = weights.shape[0]
    w = thirds(weights)
    first, second, third = w[:n], w[n : 2 * n], w[2 * n :]
    none = jnp.zeros_like(first)
    left = jnp.concatenate(
        [
            jnp.concatenate([first, first, first], axis=1),
            jnp.concatenate([second, second, none], axis=1),
            jnp.concatenate([third, none, none], axis=1),
        ],
        axis=0,
    )
    fetch.wait()
    chunks = sems.shape[0] - 1
    wide = out_ref.shape[1] // chunks
    copies = []
    for i in range(chunks):
        for k in range(i * wide, (i + 1) * wide, STEP):
            got = bf16_dot(left, thirds(panel_held[:, k : k + STEP]))
            out_held[:, k : k + STEP] = (got[2 * n :] + got[n : 2 * n]) + got[:n]
        part = pl.ds(i * wide, wide)
        copies.append(pltpu.make_async_copy(out_held.at[:, part], out_ref.at[:, part], sems.at[i]))
        copies[-1].start()
    for copy in copies:
        copy.wait()


def float_array(*shape):
    return jax.ShapeDtypeStruct(shape, jnp.float32)


def relayout(capacity, stored, slot, other, chip, position):
    n = chip.shape[0]
    store = lax.axis_size("store")
    chips, columns = store // CORES, other.shape[1]
    z, _ = place()
    far, near = chips // 2, (1, chips - 1)
    rest = (*near, 0)
    block, parts = picked_first(far, rest, chips, capacity, stored, slot, other)
    blocks = {far: send(block, far)}
    others = swap(parts)
    for i, d in enumerate(rest):
        made = picked(d, HALVES if d else 1, chips, capacity, stored, slot, others, i, block)
        block = made[0]
        blocks[d] = [send(half, d) for half in made] if d else block
    distance = lax.rem(z - chip + chips, chips)
    first, last = (0, far), near

    def selector(distances):
        source = sum(jnp.where(distance == d, i + 1, 0) for i, d in enumerate(distances)) - 1
        source = jnp.where(source < 0, -(QUARTERS * capacity), source * QUARTERS * capacity + position)
        source = source[None, :] + jnp.arange(QUARTERS)[:, None] * capacity
        hit = source.reshape(-1)[:, None] == jnp.arange(len(distances) * QUARTERS * capacity)[None, :]
        return jnp.tile(hit.astype(jnp.bfloat16), (1, 3))

    def in_order(size, parts, selector, *ready):
        return pl.pallas_call(
            lambda *refs: order_kernel(len(parts), *refs),
            out_shape=float_array(QUARTERS * n, size),
            compiler_params=BIG,
        )(*parts, selector, *ready)

    wide = columns // QUARTERS
    ready = in_order(wide, [blocks[d] for d in first], selector(first))
    last = selector(last)
    done = in_order(wide // HALVES, [blocks[d][0] for d in near], last, ready)
    shape = blocks[near[0]][1].shape
    return pl.pallas_call(
        lambda *refs: gram_kernel(capacity == CORES * stored.shape[0], *refs),
        out_shape=(float_array(n, columns), float_array(store, n // 2 + 8, 2 * n)),
        in_specs=[ANY, ANY, VMEM, VMEM, VMEM],
        out_specs=(ANY, VMEM),
        scratch_shapes=[
            pltpu.VMEM((2, *shape), jnp.float32),
            pltpu.VMEM((n, columns), jnp.float32),
            pltpu.SemaphoreType.DMA((2, QUARTERS)),
        ],
        compiler_params=BIG,
    )(*[blocks[d][1] for d in near], last, done, ready)


def per_device(stored, snap_slot):
    n = snap_slot.shape[0]
    slots = stored.shape[0]
    store, rows = lax.axis_size("store"), lax.axis_size("rows")
    columns, chips = stored.shape[1] // store, store // CORES
    part = pl.pallas_call(
        lambda *refs: part_kernel(chips // 2, chips, *refs),
        out_shape=float_array(slots, columns),
        in_specs=[HBM],
        scratch_shapes=[pltpu.SemaphoreType.DMA(())],
        compiler_params=BIG,
    )(stored)
    other = swap(part)
    chip = snap_slot // (slots * CORES)
    same = chip[:, None] == chip[None, :]
    position = jnp.sum((same & (snap_slot[None, :] < snap_slot[:, None])).astype(jnp.int32), axis=1)
    most = jnp.max(position) + 1
    capacities = (22, 24, 26, 32)
    choice = sum((most > c).astype(jnp.int32) for c in capacities[:-1])
    branches = [lambda *args, c=c: relayout(c, *args) for c in capacities]
    panel, pairs = lax.switch(choice, branches, stored, snap_slot[None, :], other, chip, position)
    pairs = lax.optimization_barrier(pairs)
    pairs = lax.all_to_all(pairs, "store", split_axis=0, concat_axis=0, tiled=True)
    pairs = pl.pallas_call(sum_kernel, out_shape=float_array(rows, *pairs.shape[1:]), compiler_params=BIG)(pairs)
    pairs = lax.all_to_all(pairs, "rows", split_axis=0, concat_axis=0, tiled=True)
    modes, factor = pl.pallas_call(
        lambda *refs: modes_kernel(columns * store * rows, *refs),
        out_shape=(float_array(n, columns), float_array(n, n)),
        in_specs=[VMEM, ANY],
        out_specs=(ANY, VMEM),
        scratch_shapes=[pltpu.VMEM((n, columns), jnp.float32)] * 2 + [pltpu.SemaphoreType.DMA((9,))],
        compiler_params=BIG,
    )(pairs, panel)
    return (modes, factor)


def solution(mesh):
    in_specs = (P("store", "rows"), P())
    out_specs = (P(None, ("rows", "store")), P())
    return jax.shard_map(
        per_device, mesh=mesh, in_specs=in_specs, out_specs=out_specs, check_vma=False
    )
```
